32 devices in a mesh: ctx: 16 (over z, y, x), ch: 2 (over core).
Axes of the slice: x: 2, y: 2, z: 4, core: 2. Of those that a mesh axis runs over, the one named last changes fastest.
Arguments:
- features: bfloat16 [6144, 4096], P('ctx', 'ch'), may hold values from -6 to 6
- proj_weight: bfloat16 [4096, 4096], P('ctx', 'ch'), may hold values from -0.09375 to 0.09375
- gate_q: bfloat16 [6144, 4096], P('ctx', 'ch'), may hold values from -6 to 6
- gate_k: bfloat16 [6144, 4096], P('ctx', 'ch'), may hold values from -6 to 6
- filter_spec: float32 [2, 32, 384, 4096], P(None, 'ctx', None, 'ch'), may hold values from -6 to 6
Outputs:
- gated: bfloat16 [6144, 4096], P('ctx', 'ch')
The draws below stay inside these ranges and needn't reach their ends.
All inputs are finite; a program needn't handle non-finite values.
Results may differ from the reference program's by a relative error of at most 0.0049.
Values may be sent and summed in bfloat16 or wider, within the bound.
No kernel may reach another device: no remote copies, remote signals or barrier semaphores. Data moves between devices by JAX's collectives and lax.ppermute only.
A program may use at most 128 MiB of HBM per device.

```python
import jax
import jax.numpy as jnp
from jax import lax

D = 4096
CHANS = 4096
TOK_DEV = 384
TOKENS = 6144
FREQ_ROWS = 32
FFT_LEN = 12288


def block_levels(rng, dims, shards, low, largest):
    def one(axis_at, blocks):
        heights = jax.random.uniform(jax.random.fold_in(jax.random.fold_in(rng, 6), axis_at), (blocks,), jnp.float32, low / len(shards), largest / len(shards))
        return jnp.repeat(jnp.exp(heights), dims[axis_at] // blocks).reshape((-1,) + (1,) * (len(dims) - axis_at - 1))

    factor_of = one(*shards[0])
    for cut in shards[1:]:
        factor_of = factor_of * one(*cut)
    return factor_of


def scatter_about(key, shape, deviation, most, shards=(), kind=jnp.bfloat16):
    gain = block_levels(key, shape, shards, -0.22, 0.18) if shards else 1.0
    array = jax.random.normal(key, shape, jnp.float32) * deviation * gain
    return jnp.minimum(jnp.maximum(array, -most), most).astype(kind)


def setup_inputs(seed: int = 0) -> dict:
    seeds = jax.random.split(jax.random.key(seed), 6)
    return {
        "features": scatter_about(seeds[0], (TOKENS, D), 1.0, 6.0, ((0, 16), (1, 2))),
        "proj_weight": scatter_about(seeds[1], (D, CHANS), D ** -0.5, 0.09375, ((0, 16), (1, 2))),
        "gate_q": scatter_about(seeds[2], (TOKENS, CHANS), 1.0, 6.0, ((0, 16), (1, 2))),
        "gate_k": scatter_about(seeds[3], (TOKENS, CHANS), 1.0, 6.0, ((0, 16), (1, 2))),
        "filter_spec": scatter_about(seeds[4], (2, FREQ_ROWS, TOK_DEV, CHANS), 1.0, 6.0, ((1, 16), (3, 2)), jnp.float32),
    }


def reference(features, proj_weight, gate_q, gate_k, filter_spec):
    projected = jnp.dot(features, proj_weight, preferred_element_type=jnp.float32)
    signal = (gate_k.astype(jnp.float32) * projected).astype(jnp.bfloat16)
    block_size = min(CHANS, 512)
    block_count = CHANS // block_size

    def one_block(block_index):
        offset = (block_index * block_size).astype(jnp.int32)
        block_signal = lax.dynamic_slice_in_dim(signal, offset, block_size, 1)
        block_spec = lax.dynamic_slice_in_dim(filter_spec, offset, block_size, 3)
        block_spec = jnp.transpose(block_spec, (0, 2, 1, 3)).reshape(2, FFT_LEN, block_size)
        padded = jnp.zeros((FFT_LEN, block_size), jnp.float32).at[:TOKENS].set(block_signal.astype(jnp.float32))
        forward = jnp.fft.fft(padded, axis=0)
        product = forward * lax.complex(block_spec[0], block_spec[1])
        return jnp.real(jnp.fft.ifft(product, axis=0))[:TOKENS]

    convolved = lax.map(one_block, jnp.arange(block_count, dtype=jnp.int32))
    convolved = jnp.transpose(convolved, (1, 0, 2)).reshape(TOKENS, CHANS)
    return (gate_q.astype(jnp.float32) * convolved).astype(jnp.bfloat16)
```

```python
import functools
import math

import jax
import jax.numpy as jnp
import numpy as np
from jax import lax
from jax.experimental import pallas as pl
from jax.experimental.pallas import tpu as pltpu
from jax.sharding import PartitionSpec as P

BF16 = jnp.bfloat16
F32 = jnp.float32
VMEM_LIMIT = 56 * 1024 * 1024
TIME_TILE = 16
FREQ_CHUNK = 4


def plane_size(ctx_size):
    size = 1
    while ctx_size % (2 * size) == 0 and 4 * size * size <= ctx_size:
        size *= 2
    return size


def best_scale(values):
    distinct, counts = np.unique(np.round(np.abs(values), 12), return_counts=True)
    best, best_error = 1.0, None
    for factor in np.linspace(1.0, 2.0, 2000, endpoint=False):
        scaled = distinct * factor
        rounded = scaled.astype(jnp.bfloat16).astype(np.float64)
        error = float((counts * (rounded - scaled) ** 2).sum()) / factor**2
        if best_error is None or error < best_error:
            best, best_error = float(factor), error
    return best


def split_table(table):
    high = table.astype(jnp.bfloat16)
    low = (table - high.astype(np.float64)).astype(jnp.bfloat16)
    return high, low


def transform_tables(slab_count, tok_rows):
    freq_count = 2 * slab_count
    length = freq_count * tok_rows
    freq = np.arange(freq_count)
    slab = np.arange(slab_count)
    fine = np.arange(TIME_TILE)
    group = np.arange(tok_rows // TIME_TILE)
    turns = (freq[:, None, None] * slab[None, None, :] % freq_count) / freq_count + (
        freq[:, None, None] * fine[None, :, None]
    ) / length
    phase = np.exp(-2j * np.pi * turns)
    slab_table = np.zeros((freq_count, 2, TIME_TILE, slab_count, TIME_TILE))
    for u in range(TIME_TILE):
        slab_table[:, 0, u, :, u] = phase[:, u].real
        slab_table[:, 1, u, :, u] = phase[:, u].imag
    slab_table = slab_table.reshape(freq_count * 2 * TIME_TILE, slab_count * TIME_TILE)
    row = np.arange(tok_rows)
    turns = (row[:, None] * row[None, :] % tok_rows) / tok_rows
    cosine, sine = np.cos(2 * np.pi * turns), np.sin(2 * np.pi * turns)
    forward_rows = np.block([[cosine, sine], [-sine, cosine]])
    scale = best_scale(forward_rows)
    forward_rows = forward_rows * scale
    coarse = np.exp(-2j * np.pi * (freq[:, None] * TIME_TILE * group[None, :] % length) / length)
    coarse = np.stack([coarse.real, coarse.imag], axis=-1)
    inverse_scale = 1.0 / (length * scale * scale)
    return {
        "slab": split_table(slab_table),
        "slab_back": split_table(slab_table.T),
        "rows": forward_rows.astype(jnp.bfloat16),
        "rows_back": forward_rows.T.astype(jnp.bfloat16),
        "coarse": coarse.astype(np.float32).reshape(-1),
        "coarse_back": (coarse * inverse_scale).astype(np.float32).reshape(-1),
    }


def convolve_kernel(
    slab_count,
    tok_rows,
    channels,
    coarse_ref,
    coarse_back_ref,
    signal_ref,
    spectrum_ref,
    slab_high_ref,
    slab_low_ref,
    back_high_ref,
    back_low_ref,
    rows_ref,
    rows_back_ref,
    out_ref,
    work_ref,
    rest_ref,
):
    freq_count = 2 * slab_count
    groups = tok_rows // TIME_TILE
    step = pl.program_id(0)
    tile = TIME_TILE

    def scalars(ref, freq, group):
        at = 2 * (freq * groups + group)
        return ref[at], ref[at + 1]

    @pl.when(step == 0)
    def _():
        @pl.loop(0, groups // 2)
        def _(pair):
            parts = []
            for half in range(2):
                start = pl.multiple_of((2 * pair + half) * tile, tile)
                piece = signal_ref[:, pl.ds(start, tile), :]
                parts.append(piece.reshape(slab_count * tile, channels))
            block = jnp.concatenate(parts, axis=1)
            summed = jnp.dot(slab_high_ref[...], block, preferred_element_type=F32)
            summed += jnp.dot(slab_low_ref[...], block, preferred_element_type=F32)
            for freq in range(freq_count):
                base = freq * 2 * tile
                for half in range(2):
                    lanes = slice(half * channels, (half + 1) * channels)
                    real = summed[base : base + tile, lanes]
                    imag = summed[base + tile : base + 2 * tile, lanes]
                    cos, sin = scalars(coarse_ref, freq, 2 * pair + half)
                    start = pl.multiple_of((2 * pair + half) * tile, tile)
                    work_ref[freq, 0, pl.ds(start, tile), :] = (real * cos - imag * sin).astype(BF16)
                    work_ref[freq, 1, pl.ds(start, tile), :] = (real * sin + imag * cos).astype(BF16)

    first = step * FREQ_CHUNK
    wide = jnp.concatenate(
        [work_ref[first + at].reshape(2 * tok_rows, channels) for at in range(FREQ_CHUNK)], axis=1
    )
    forward = jnp.dot(rows_ref[...], wide, preferred_element_type=F32)
    products = []
    for at in range(FREQ_CHUNK):
        lanes = slice(at * channels, (at + 1) * channels)
        real, imag = forward[:tok_rows, lanes], forward[tok_rows:, lanes]
        spec_real = spectrum_ref[at, 0].astype(F32)
        spec_imag = spectrum_ref[at, 1].astype(F32)
        products.append(
            jnp.concatenate(
                [
                    (spec_real * real - spec_imag * imag).astype(BF16),
                    (spec_real * imag + spec_imag * real).astype(BF16),
                ],
                axis=0,
            )
        )
    inverse = jnp.dot(
        rows_back_ref[...], jnp.concatenate(products, axis=1), preferred_element_type=F32
    )
    for at in range(FREQ_CHUNK):
        lanes = slice(at * channels, (at + 1) * channels)
        for group in range(groups):
            rows = slice(group * tile, (group + 1) * tile)
            real = inverse[rows, lanes]
            imag = inverse[tok_rows + group * tile : tok_rows + (group + 1) * tile, lanes]
            cos, sin = scalars(coarse_back_ref, first + at, group)
            for part, value in enumerate((real * cos + imag * sin, imag * cos - real * sin)):
                high = value.astype(BF16)
                work_ref[first + at, part, rows, :] = high
                rest_ref[first + at, part, rows, :] = (value - high.astype(F32)).astype(BF16)

    @pl.when(step == pl.num_programs(0) - 1)
    def _():
        @pl.loop(0, groups // 2)
        def _(pair):
            highs, lows = [], []
            for half in range(2):
                start = pl.multiple_of((2 * pair + half) * tile, tile)
                depth = freq_count * 2 * tile
                highs.append(work_ref[:, :, pl.ds(start, tile), :].reshape(depth, channels))
                lows.append(rest_ref[:, :, pl.ds(start, tile), :].reshape(depth, channels))
            high = jnp.concatenate(highs, axis=1)
            low = jnp.concatenate(lows, axis=1)
            total = jnp.dot(back_high_ref[...], high, preferred_element_type=F32)
            total += jnp.dot(back_low_ref[...], high, preferred_element_type=F32)
            total += jnp.dot(back_high_ref[...], low, preferred_element_type=F32)
            for half in range(2):
                start = pl.multiple_of((2 * pair + half) * tile, tile)
                lanes = slice(half * channels, (half + 1) * channels)
                out_ref[:, pl.ds(start, tile), :] = (
                    total[:, lanes].reshape(slab_count, tile, channels).astype(BF16)
                )


def convolve_fused(signal, spectrum, tables):
    slab_count, tok_rows, channels = signal.shape
    freq_count = 2 * slab_count
    whole = lambda array: pl.BlockSpec(array.shape, lambda i: (0,) * array.ndim)
    scalar = pl.BlockSpec(memory_space=pltpu.SMEM)
    consts = [
        *tables["slab"],
        *tables["slab_back"],
        tables["rows"],
        tables["rows_back"],
    ]
    consts = [jnp.asarray(c) for c in consts]
    flops = 2 * freq_count * channels * (2 * (2 * tok_rows) ** 2 + 5 * 2 * tok_rows * slab_count * TIME_TILE)
    return pl.pallas_call(
        functools.partial(convolve_kernel, slab_count, tok_rows, channels),
        grid=(freq_count // FREQ_CHUNK,),
        in_specs=[
            scalar,
            scalar,
            whole(signal),
            pl.BlockSpec((FREQ_CHUNK, 2, tok_rows, channels), lambda i: (i, 0, 0, 0)),
            *[whole(c) for c in consts],
        ],
        out_specs=whole(signal),
        out_shape=jax.ShapeDtypeStruct(signal.shape, BF16),
        scratch_shapes=[
            pltpu.VMEM((freq_count, 2, tok_rows, channels), BF16),
            pltpu.VMEM((freq_count, 2, tok_rows, channels), BF16),
        ],
        compiler_params=pltpu.CompilerParams(
            dimension_semantics=("arbitrary",), vmem_limit_bytes=VMEM_LIMIT
        ),
        cost_estimate=pl.CostEstimate(
            flops=flops, bytes_accessed=2 * spectrum.size + 4 * signal.size, transcendentals=0
        ),
        name="convolve",
    )(
        jnp.asarray(tables["coarse"]),
        jnp.asarray(tables["coarse_back"]),
        signal,
        spectrum,
        *consts,
    )


def convolve_plain(signal, spectrum):
    slab_count, tok_rows, channels = signal.shape
    freq_count = 2 * slab_count
    length = freq_count * tok_rows

    def phase(left, right, modulus):
        turns = (left[:, None] * right[None, :] % modulus).astype(F32) * (2.0 * math.pi / modulus)
        return jnp.cos(turns), jnp.sin(turns)

    dot = functools.partial(jnp.einsum, precision=lax.Precision.HIGH, preferred_element_type=F32)
    freq = jnp.arange(freq_count, dtype=jnp.int32)
    slab = jnp.arange(slab_count, dtype=jnp.int32)
    row = jnp.arange(tok_rows, dtype=jnp.int32)
    slab_cos, slab_sin = phase(freq, slab, freq_count)
    turn_cos, turn_sin = (part[:, :, None] for part in phase(freq, row, length))
    row_cos, row_sin = phase(row, row, tok_rows)
    values = signal.astype(F32)
    real, imag = dot("ks,stc->ktc", slab_cos, values), -dot("ks,stc->ktc", slab_sin, values)
    real, imag = real * turn_cos + imag * turn_sin, imag * turn_cos - real * turn_sin
    real, imag = (
        dot("jt,ktc->kjc", row_cos, real) + dot("jt,ktc->kjc", row_sin, imag),
        dot("jt,ktc->kjc", row_cos, imag) - dot("jt,ktc->kjc", row_sin, real),
    )
    spec_real, spec_imag = spectrum[:, 0].astype(F32), spectrum[:, 1].astype(F32)
    real, imag = real * spec_real - imag * spec_imag, imag * spec_real + real * spec_imag
    real, imag = (
        dot("jt,ktc->kjc", row_cos, real) - dot("jt,ktc->kjc", row_sin, imag),
        dot("jt,ktc->kjc", row_cos, imag) + dot("jt,ktc->kjc", row_sin, real),
    )
    real, imag = real * turn_cos - imag * turn_sin, imag * turn_cos + real * turn_sin
    values = dot("ks,ktc->stc", slab_cos, real) - dot("ks,ktc->stc", slab_sin, imag)
    return (values / length).astype(BF16)


def per_device(tables, features, proj_weight, gate_q, gate_k, filter_spec):
    ctx_size = lax.axis_size("ctx")
    ch_size = lax.axis_size("ch")
    plane = plane_size(ctx_size)
    lines = ctx_size // plane
    me = lax.axis_index("ctx")
    ch_me = lax.axis_index("ch")
    line_at, plane_at = me // plane, me % plane
    tok_rows, feat_cols = features.shape
    weight_rows, group_channels = proj_weight.shape
    wide = group_channels // plane
    channels = wide // lines
    freq_local = filter_spec.shape[1]

    plane_groups = [[z * plane + p for p in range(plane)] for z in range(lines)]
    line_groups = [[z * plane + p for z in range(lines)] for p in range(plane)]
    plane_perm = lambda d: [(i, i // plane * plane + (i % plane ^ d)) for i in range(ctx_size)]
    up = [(i, i + plane) for i in range(ctx_size - plane)]
    down = [(i + plane, i) for i in range(ctx_size - plane)]

    weight = proj_weight.reshape(weight_rows, plane, wide).transpose(1, 0, 2)
    weight = lax.all_to_all(weight, "ctx", 0, 0, tiled=True, axis_index_groups=plane_groups)
    weight = weight.reshape(plane * weight_rows, wide)
    from_below, from_above = [weight], [weight]
    for _ in range(lines - 1):
        from_below.append(lax.ppermute(from_below[-1], "ctx", up))
        from_above.append(lax.ppermute(from_above[-1], "ctx", down))

    feature_pieces = [features] + [
        lax.ppermute(features, "ctx", plane_perm(d)) for d in range(1, plane)
    ]
    gate_blocks = gate_k.reshape(tok_rows, plane, wide)
    gate_pieces = []
    for d in range(plane):
        block = lax.dynamic_index_in_dim(gate_blocks, plane_at ^ d, 1, keepdims=False)
        gate_pieces.append(block if d == 0 else lax.ppermute(block, "ctx", plane_perm(d)))

    spec = filter_spec.reshape(2, freq_local, tok_rows, plane, lines, channels)
    spec = spec.transpose(4, 3, 1, 0, 2, 5).astype(BF16)
    spec = spec.reshape(ctx_size, freq_local, 2, tok_rows, channels)
    spec = lax.all_to_all(spec, "ctx", 0, 0, tiled=True)
    spec = spec.reshape(ctx_size * freq_local, 2, tok_rows, channels)

    ordered = [weight] + [
        jnp.where(line_at + m < lines, from_above[m], from_below[lines - m]) for m in range(1, lines)
    ]
    stacked = jnp.stack(ordered)
    take = jnp.mod(jnp.arange(lines) - line_at, lines)
    full_weight = stacked[take].reshape(ch_size, feat_cols, wide)

    signals = []
    for d in range(plane):
        total = None
        for e in range(ch_size):
            piece = feature_pieces[d]
            if e:
                piece = lax.ppermute(
                    piece, "ch", [(i, (i + e) % ch_size) for i in range(ch_size)]
                )
            half = lax.dynamic_index_in_dim(
                full_weight, (ch_me - e) % ch_size, 0, keepdims=False
            )
            term = jnp.dot(piece, half, preferred_element_type=F32)
            total = term if total is None else total + term
        signals.append((gate_pieces[d].astype(F32) * total).astype(BF16))
    signal = jnp.stack(signals)
    signal = signal[jnp.arange(plane) ^ plane_at]
    signal = signal.reshape(plane, tok_rows, lines, channels).transpose(2, 0, 1, 3)
    signal = lax.all_to_all(signal, "ctx", 0, 0, tiled=True, axis_index_groups=line_groups)
    signal = signal.reshape(ctx_size, tok_rows, channels)

    if channels % 128 == 0:
        convolved = convolve_fused(signal, spec, tables)
    else:
        convolved = convolve_plain(signal, spec)
    returned = lax.all_to_all(convolved, "ctx", 0, 0, tiled=True)
    returned = returned.reshape(lines, plane, tok_rows, channels).transpose(2, 1, 0, 3)
    returned = returned.reshape(tok_rows, group_channels)
    return (gate_q.astype(F32) * returned.astype(F32)).astype(BF16)


def solution(mesh):
    ctx_size = mesh.shape["ctx"]

    def whole(features, proj_weight, gate_q, gate_k, filter_spec):
        tables = transform_tables(ctx_size, features.shape[0] // ctx_size)
        return jax.shard_map(
            functools.partial(per_device, tables),
            mesh=mesh,
            in_specs=(
                P("ctx", "ch"),
                P("ctx", "ch"),
                P("ctx", "ch"),
                P("ctx", "ch"),
                P(None, "ctx", None, "ch"),
            ),
            out_specs=P("ctx", "ch"),
            check_vma=False,
        )(features, proj_weight, gate_q, gate_k, filter_spec)

    return whole
```

```python
import functools
import math

import jax
import jax.numpy as jnp
import numpy as np
from jax import lax
from jax.experimental import pallas as pl
from jax.experimental.pallas import tpu as pltpu
from jax.sharding import PartitionSpec as P

BF16 = jnp.bfloat16
F32 = jnp.float32
VMEM_LIMIT = 56 * 1024 * 1024
TIME_TILE = 16
FREQ_CHUNK = 4


def plane_size(ctx_size):
    size = 1
    while ctx_size % (2 * size) == 0 and 4 * size * size <= ctx_size:
        size *= 2
    return size


def best_scale(values):
    distinct, counts = np.unique(np.round(np.abs(values), 12), return_counts=True)
    best, best_error = 1.0, None
    for factor in np.linspace(1.0, 2.0, 2000, endpoint=False):
        scaled = distinct * factor
        rounded = scaled.astype(jnp.bfloat16).astype(np.float64)
        error = float((counts * (rounded - scaled) ** 2).sum()) / factor**2
        if best_error is None or error < best_error:
            best, best_error = float(factor), error
    return best


def split_table(table):
    high = table.astype(jnp.bfloat16)
    low = (table - high.astype(np.float64)).astype(jnp.bfloat16)
    return high, low


def transform_tables(slab_count, tok_rows, first, stride):
    freq_count = 2 * slab_count
    length = freq_count * tok_rows
    freq = np.arange(first, freq_count, stride)
    slab = np.arange(slab_count)
    fine = np.arange(TIME_TILE)
    group = np.arange(tok_rows // TIME_TILE)
    turns = (freq[:, None, None] * slab[None, None, :] % freq_count) / freq_count + (
        freq[:, None, None] * fine[None, :, None]
    ) / length
    phase = np.exp(-2j * np.pi * turns)
    slab_table = np.zeros((len(freq), 2, TIME_TILE, slab_count, TIME_TILE))
    for u in range(TIME_TILE):
        slab_table[:, 0, u, :, u] = phase[:, u].real
        slab_table[:, 1, u, :, u] = phase[:, u].imag
    slab_table = slab_table.reshape(len(freq) * 2 * TIME_TILE, slab_count * TIME_TILE)
    row = np.arange(tok_rows)
    turns = (row[:, None] * row[None, :] % tok_rows) / tok_rows
    cosine, sine = np.cos(2 * np.pi * turns), np.sin(2 * np.pi * turns)
    forward_rows = np.block([[cosine, sine], [-sine, cosine]])
    scale = best_scale(forward_rows)
    forward_rows = forward_rows * scale
    coarse = np.exp(-2j * np.pi * (freq[:, None] * TIME_TILE * group[None, :] % length) / length)
    coarse = np.stack([coarse.real, coarse.imag], axis=-1)
    inverse_scale = 1.0 / (length * scale * scale)
    return {
        "slab": split_table(slab_table),
        "slab_back": split_table(slab_table.T),
        "rows": forward_rows.astype(jnp.bfloat16),
        "rows_back": forward_rows.T.astype(jnp.bfloat16),
        "coarse": coarse.astype(np.float32).reshape(-1),
        "coarse_back": (coarse * inverse_scale).astype(np.float32).reshape(-1),
    }


def coarse_turn(ref, groups, freq, group):
    at = 2 * (freq * groups + group)
    return ref[at], ref[at + 1]


def slab_stage(coarse_ref, signal_ref, high_ref, low_ref, work_ref):
    slab_count, tok_rows, channels = signal_ref.shape
    freq_count = work_ref.shape[0]
    groups = tok_rows // TIME_TILE
    tile = TIME_TILE

    @pl.loop(0, groups // 2)
    def _(pair):
        parts = []
        for half in range(2):
            start = pl.multiple_of((2 * pair + half) * tile, tile)
            piece = signal_ref[:, pl.ds(start, tile), :]
            parts.append(piece.reshape(slab_count * tile, channels))
        block = jnp.concatenate(parts, axis=1)
        summed = jnp.dot(high_ref[...], block, preferred_element_type=F32)
        summed += jnp.dot(low_ref[...], block, preferred_element_type=F32)
        for freq in range(freq_count):
            base = freq * 2 * tile
            for half in range(2):
                lanes = slice(half * channels, (half + 1) * channels)
                real = summed[base : base + tile, lanes]
                imag = summed[base + tile : base + 2 * tile, lanes]
                cos, sin = coarse_turn(coarse_ref, groups, freq, 2 * pair + half)
                start = pl.multiple_of((2 * pair + half) * tile, tile)
                work_ref[freq, 0, pl.ds(start, tile), :] = (real * cos - imag * sin).astype(BF16)
                work_ref[freq, 1, pl.ds(start, tile), :] = (real * sin + imag * cos).astype(BF16)


def rows_stage(work_ref, rows_ref, first):
    _, _, tok_rows, channels = work_ref.shape
    wide = [work_ref[first + at].reshape(2 * tok_rows, channels) for at in range(FREQ_CHUNK)]
    return jnp.dot(rows_ref[...], jnp.concatenate(wide, axis=1), preferred_element_type=F32)


def product_and_back(forward, spectrum_ref, rows_back_ref, coarse_back_ref, work_ref, rest_ref, first):
    _, _, tok_rows, channels = work_ref.shape
    groups = tok_rows // TIME_TILE
    products = []
    for at in range(FREQ_CHUNK):
        real, imag = forward(at)
        spec_real = spectrum_ref[at, 0].astype(F32)
        spec_imag = spectrum_ref[at, 1].astype(F32)
        products.append(
            jnp.concatenate(
                [
                    (spec_real * real - spec_imag * imag).astype(BF16),
                    (spec_real * imag + spec_imag * real).astype(BF16),
                ],
                axis=0,
            )
        )
    inverse = jnp.dot(
        rows_back_ref[...], jnp.concatenate(products, axis=1), preferred_element_type=F32
    )
    for at in range(FREQ_CHUNK):
        lanes = slice(at * channels, (at + 1) * channels)
        for group in range(groups):
            rows = slice(group * TIME_TILE, (group + 1) * TIME_TILE)
            real = inverse[rows, lanes]
            imag = inverse[tok_rows + rows.start : tok_rows + rows.stop, lanes]
            cos, sin = coarse_turn(coarse_back_ref, groups, first + at, group)
            for part, value in enumerate((real * cos + imag * sin, imag * cos - real * sin)):
                high = value.astype(BF16)
                work_ref[first + at, part, rows, :] = high
                rest_ref[first + at, part, rows, :] = (value - high.astype(F32)).astype(BF16)


def slab_back_stage(work_ref, rest_ref, high_ref, low_ref, others, out_ref):
    slab_count, tok_rows, channels = out_ref.shape
    freq_count = work_ref.shape[0]
    tile = TIME_TILE
    depth = freq_count * 2 * tile

    @pl.loop(0, tok_rows // tile // 2)
    def _(pair):
        highs, lows = [], []
        for half in range(2):
            start = pl.multiple_of((2 * pair + half) * tile, tile)
            highs.append(work_ref[:, :, pl.ds(start, tile), :].reshape(depth, channels))
            lows.append(rest_ref[:, :, pl.ds(start, tile), :].reshape(depth, channels))
        high = jnp.concatenate(highs, axis=1)
        low = jnp.concatenate(lows, axis=1)
        total = jnp.dot(high_ref[...], high, preferred_element_type=F32)
        total += jnp.dot(low_ref[...], high, preferred_element_type=F32)
        total += jnp.dot(high_ref[...], low, preferred_element_type=F32)
        for half in range(2):
            start = pl.multiple_of((2 * pair + half) * tile, tile)
            lanes = slice(half * channels, (half + 1) * channels)
            value = total[:, lanes].reshape(slab_count, tile, channels)
            for other in others:
                value += other[:, pl.ds(start, tile), :]
            out_ref[:, pl.ds(start, tile), :] = value.astype(out_ref.dtype)


def convolve_kernel(
    coarse_ref,
    coarse_back_ref,
    signal_ref,
    spectrum_ref,
    slab_high_ref,
    slab_low_ref,
    back_high_ref,
    back_low_ref,
    rows_ref,
    rows_back_ref,
    out_ref,
    work_ref,
    rest_ref,
):
    _, tok_rows, channels = signal_ref.shape
    step = pl.program_id(0)

    @pl.when(step == 0)
    def _():
        slab_stage(coarse_ref, signal_ref, slab_high_ref, slab_low_ref, work_ref)

    first = step * FREQ_CHUNK
    transformed = rows_stage(work_ref, rows_ref, first)

    def forward(at):
        lanes = slice(at * channels, (at + 1) * channels)
        return transformed[:tok_rows, lanes], transformed[tok_rows:, lanes]

    product_and_back(forward, spectrum_ref, rows_back_ref, coarse_back_ref, work_ref, rest_ref, first)

    @pl.when(step == pl.num_programs(0) - 1)
    def _():
        slab_back_stage(work_ref, rest_ref, back_high_ref, back_low_ref, [], out_ref)


def forward_kernel(coarse_ref, signal_ref, slab_high_ref, slab_low_ref, rows_ref, out_ref, work_ref):
    _, tok_rows, channels = signal_ref.shape
    step = pl.program_id(0)

    @pl.when(step == 0)
    def _():
        slab_stage(coarse_ref, signal_ref, slab_high_ref, slab_low_ref, work_ref)

    transformed = rows_stage(work_ref, rows_ref, step * FREQ_CHUNK)
    for at in range(FREQ_CHUNK):
        lanes = slice(at * channels, (at + 1) * channels)
        out_ref[at, 0] = transformed[:tok_rows, lanes]
        out_ref[at, 1] = transformed[tok_rows:, lanes]


def inverse_kernel(
    coarse_back_ref,
    forward_ref,
    spectrum_ref,
    back_high_ref,
    back_low_ref,
    rows_back_ref,
    other_ref,
    out_ref,
    work_ref,
    rest_ref,
):
    step = pl.program_id(0)

    def forward(at):
        return forward_ref[at, 0], forward_ref[at, 1]

    product_and_back(
        forward, spectrum_ref, rows_back_ref, coarse_back_ref, work_ref, rest_ref, step * FREQ_CHUNK
    )

    @pl.when(step == pl.num_programs(0) - 1)
    def _():
        slab_back_stage(work_ref, rest_ref, back_high_ref, back_low_ref, [other_ref], out_ref)


def whole_block(array):
    return pl.BlockSpec(array.shape, lambda i: (0,) * array.ndim)


def frequency_call(kernel, name, freq_count, operands, out_shape, out_blocked, scratch, flops):
    arrays, specs = [], []

    def blocked(shape):
        return pl.BlockSpec((FREQ_CHUNK,) + shape[1:], lambda i: (i,) + (0,) * (len(shape) - 1))

    for array, kind in operands:
        array = jnp.asarray(array)
        arrays.append(array)
        if kind == "scalar":
            specs.append(pl.BlockSpec(memory_space=pltpu.SMEM))
        else:
            specs.append(blocked(array.shape) if kind == "blocked" else whole_block(array))
    moved = sum(a.size * a.dtype.itemsize for a in arrays)
    return pl.pallas_call(
        kernel,
        grid=(freq_count // FREQ_CHUNK,),
        in_specs=specs,
        out_specs=blocked(out_shape.shape) if out_blocked else whole_block(out_shape),
        out_shape=out_shape,
        scratch_shapes=scratch,
        compiler_params=pltpu.CompilerParams(
            dimension_semantics=("arbitrary",), vmem_limit_bytes=VMEM_LIMIT
        ),
        cost_estimate=pl.CostEstimate(flops=flops, bytes_accessed=moved, transcendentals=0),
        name=name,
    )(*arrays)


def convolve_fused(signal, spectra, tables):
    slab_count, tok_rows, channels = signal.shape
    freq_count = spectra[0].shape[0]
    rows_flops = 2 * freq_count * channels * (2 * tok_rows) ** 2
    slab_flops = 4 * freq_count * channels * tok_rows * slab_count * TIME_TILE
    work = pltpu.VMEM((freq_count, 2, tok_rows, channels), BF16)
    total = None
    for spectrum, table in zip(spectra[:-1], tables[:-1]):
        part = frequency_call(
            convolve_kernel,
            "convolve",
            freq_count,
            [
                (table["coarse"], "scalar"),
                (table["coarse_back"], "scalar"),
                (signal, "whole"),
                (spectrum, "blocked"),
                *[(t, "whole") for t in table["slab"]],
                *[(t, "whole") for t in table["slab_back"]],
                (table["rows"], "whole"),
                (table["rows_back"], "whole"),
            ],
            jax.ShapeDtypeStruct(signal.shape, F32),
            False,
            [work, work],
            2 * rows_flops + 5 * slab_flops,
        )
        total = part if total is None else total + part
    if total is None:
        total = jnp.zeros(signal.shape, F32)
    table = tables[-1]
    forward = frequency_call(
        forward_kernel,
        "forward",
        freq_count,
        [
            (table["coarse"], "scalar"),
            (signal, "whole"),
            *[(t, "whole") for t in table["slab"]],
            (table["rows"], "whole"),
        ],
        jax.ShapeDtypeStruct((freq_count, 2, tok_rows, channels), F32),
        True,
        [work],
        rows_flops + 2 * slab_flops,
    )
    return frequency_call(
        inverse_kernel,
        "inverse",
        freq_count,
        [
            (table["coarse_back"], "scalar"),
            (forward, "blocked"),
            (spectra[-1], "blocked"),
            *[(t, "whole") for t in table["slab_back"]],
            (table["rows_back"], "whole"),
            (total, "whole"),
        ],
        jax.ShapeDtypeStruct(signal.shape, BF16),
        False,
        [work, work],
        rows_flops + 3 * slab_flops,
    )


def spread_kernel(lines, channels, values_ref, out_ref):
    for line in range(lines):
        out_ref[line, 0, 0] = values_ref[0, 0, :, line * channels : (line + 1) * channels].astype(BF16)


def spread_spectrum(filter_spec, at, plane, lines):
    parts, _, tok_rows, group_channels = filter_spec.shape
    channels = group_channels // (plane * lines)
    if channels % 128:
        spec = filter_spec[:, at].reshape(parts, tok_rows, plane, lines, channels)
        spec = spec.transpose(3, 2, 0, 1, 4).astype(BF16)
    else:
        spec = pl.pallas_call(
            functools.partial(spread_kernel, lines, channels),
            grid=(parts, plane),
            in_specs=[
                pl.BlockSpec((1, 1, tok_rows, lines * channels), lambda i, j: (i, at, 0, j))
            ],
            out_specs=pl.BlockSpec((lines, 1, 1, tok_rows, channels), lambda i, j: (0, j, i, 0, 0)),
            out_shape=jax.ShapeDtypeStruct((lines, plane, parts, tok_rows, channels), BF16),
            compiler_params=pltpu.CompilerParams(
                dimension_semantics=("arbitrary", "arbitrary"), vmem_limit_bytes=VMEM_LIMIT
            ),
            cost_estimate=pl.CostEstimate(
                flops=0, bytes_accessed=6 * parts * tok_rows * group_channels, transcendentals=0
            ),
            name="spread_spectrum",
        )(filter_spec)
    return spec.reshape(plane * lines, parts, tok_rows, channels)


def gate_kernel(lines, channels, values_ref, gate_ref, out_ref):
    for line in range(lines):
        lanes = slice(line * channels, (line + 1) * channels)
        value = gate_ref[:, lanes].astype(F32) * values_ref[line, 0].astype(F32)
        out_ref[:, lanes] = value.astype(BF16)


def gate_output(returned, gate_q, plane, lines):
    _, tok_rows, channels = returned.shape
    returned = returned.reshape(lines, plane, tok_rows, channels)
    if channels % 128:
        returned = returned.transpose(2, 1, 0, 3).reshape(gate_q.shape)
        return (gate_q.astype(F32) * returned.astype(F32)).astype(BF16)
    flat = pl.BlockSpec((tok_rows, lines * channels), lambda i: (0, i))
    return pl.pallas_call(
        functools.partial(gate_kernel, lines, channels),
        grid=(plane,),
        in_specs=[pl.BlockSpec((lines, 1, tok_rows, channels), lambda i: (0, i, 0, 0)), flat],
        out_specs=flat,
        out_shape=jax.ShapeDtypeStruct(gate_q.shape, BF16),
        compiler_params=pltpu.CompilerParams(
            dimension_semantics=("arbitrary",), vmem_limit_bytes=VMEM_LIMIT
        ),
        cost_estimate=pl.CostEstimate(
            flops=gate_q.size, bytes_accessed=6 * gate_q.size, transcendentals=0
        ),
        name="gate_output",
    )(returned, gate_q)


def convolve_plain(signal, spectrum):
    slab_count, tok_rows, channels = signal.shape
    freq_count = 2 * slab_count
    length = freq_count * tok_rows

    def phase(left, right, modulus):
        turns = (left[:, None] * right[None, :] % modulus).astype(F32) * (2.0 * math.pi / modulus)
        return jnp.cos(turns), jnp.sin(turns)

    dot = functools.partial(jnp.einsum, precision=lax.Precision.HIGH, preferred_element_type=F32)
    freq = jnp.arange(freq_count, dtype=jnp.int32)
    slab = jnp.arange(slab_count, dtype=jnp.int32)
    row = jnp.arange(tok_rows, dtype=jnp.int32)
    slab_cos, slab_sin = phase(freq, slab, freq_count)
    turn_cos, turn_sin = (part[:, :, None] for part in phase(freq, row, length))
    row_cos, row_sin = phase(row, row, tok_rows)
    values = signal.astype(F32)
    real, imag = dot("ks,stc->ktc", slab_cos, values), -dot("ks,stc->ktc", slab_sin, values)
    real, imag = real * turn_cos + imag * turn_sin, imag * turn_cos - real * turn_sin
    real, imag = (
        dot("jt,ktc->kjc", row_cos, real) + dot("jt,ktc->kjc", row_sin, imag),
        dot("jt,ktc->kjc", row_cos, imag) - dot("jt,ktc->kjc", row_sin, real),
    )
    spec_real, spec_imag = spectrum[:, 0].astype(F32), spectrum[:, 1].astype(F32)
    real, imag = real * spec_real - imag * spec_imag, imag * spec_real + real * spec_imag
    real, imag = (
        dot("jt,ktc->kjc", row_cos, real) - dot("jt,ktc->kjc", row_sin, imag),
        dot("jt,ktc->kjc", row_cos, imag) + dot("jt,ktc->kjc", row_sin, real),
    )
    real, imag = real * turn_cos - imag * turn_sin, imag * turn_cos + real * turn_sin
    values = dot("ks,ktc->stc", slab_cos, real) - dot("ks,ktc->stc", slab_sin, imag)
    return (values / length).astype(BF16)


def after(values, earlier):
    values, earlier = list(values), list(earlier)
    anywhere = pl.BlockSpec(memory_space=pl.ANY)
    return pl.pallas_call(
        lambda *refs: None,
        in_specs=[anywhere] * (len(values) + len(earlier)),
        out_specs=[anywhere] * len(values),
        out_shape=[jax.ShapeDtypeStruct(v.shape, v.dtype) for v in values],
        input_output_aliases={i: i for i in range(len(values))},
        cost_estimate=pl.CostEstimate(flops=0, bytes_accessed=0, transcendentals=0),
        name="after",
    )(*values, *earlier)


def per_device(tables, features, proj_weight, gate_q, gate_k, filter_spec):
    ctx_size = lax.axis_size("ctx")
    ch_size = lax.axis_size("ch")
    plane = plane_size(ctx_size)
    lines = ctx_size // plane
    me = lax.axis_index("ctx")
    ch_me = lax.axis_index("ch")
    line_at, plane_at = me // plane, me % plane
    tok_rows, feat_cols = features.shape
    weight_rows, group_channels = proj_weight.shape
    wide = group_channels // plane
    channels = wide // lines
    freq_local = filter_spec.shape[1]
    tie = after if channels % 128 == 0 else lambda values, earlier: values

    plane_groups = [[z * plane + p for p in range(plane)] for z in range(lines)]
    line_groups = [[z * plane + p for z in range(lines)] for p in range(plane)]
    onward = [(i, (i + plane) % ctx_size) for i in range(ctx_size)]

    def swap(value, d):
        perm = [(i, i // plane * plane + (i % plane ^ d)) for i in range(ctx_size)]
        return lax.ppermute(value, "ctx", perm)

    def other_core(value, e):
        return lax.ppermute(value, "ch", [(i, (i + e) % ch_size) for i in range(ch_size)])

    weight = proj_weight.reshape(weight_rows, plane, wide).transpose(1, 0, 2)
    weight = lax.all_to_all(weight, "ctx", 0, 0, tiled=True, axis_index_groups=plane_groups)
    along = [weight.reshape(plane * weight_rows, wide)]
    spread = [spread_spectrum(filter_spec, at, plane, lines) for at in range(freq_local)]
    for step in range(1, lines):
        if 0 < step - 1 < freq_local + 1:
            along[-1] = tie(along[-1:], [spread[step - 2]])[0]
        along.append(lax.ppermute(along[-1], "ctx", onward))
    take = jnp.mod(line_at - jnp.arange(lines), lines)
    full_weight = jnp.stack(along)[take].reshape(ch_size, feat_cols, wide)

    plane_features = lax.all_gather(
        features, "ctx", axis=0, tiled=True, axis_index_groups=plane_groups
    )

    gate_blocks = gate_k.reshape(tok_rows, plane, wide)
    gate_pieces = [
        lax.dynamic_index_in_dim(gate_blocks, plane_at ^ d, 1, keepdims=False) for d in range(plane)
    ]
    gate_pieces = tie(gate_pieces, along[-1:])
    gate_pieces = [swap(piece, d) if d else piece for d, piece in enumerate(gate_pieces)]

    first = tie(spread[:1], along[-1:])
    spectra = [lax.all_to_all(first[0], "ctx", 0, 0, tiled=True)]

    plane_features = tie([plane_features], along[-1:])[0]
    projected = None
    for e in range(ch_size):
        piece = other_core(plane_features, e) if e else plane_features
        weights = lax.dynamic_index_in_dim(full_weight, (ch_me - e) % ch_size, 0, keepdims=False)
        term = jnp.dot(piece, weights, preferred_element_type=F32)
        projected = term if projected is None else projected + term
    projected = projected.reshape(plane, tok_rows, wide)
    gate_pieces = tie(gate_pieces, [projected])
    plane_gate = jnp.stack(gate_pieces)[jnp.arange(plane) ^ plane_at]
    signal = (plane_gate.astype(F32) * projected).astype(BF16)
    signal = signal.reshape(plane, tok_rows, lines, channels).transpose(2, 0, 1, 3)
    signal = tie([signal], spectra)[0]
    signal = lax.all_to_all(signal, "ctx", 0, 0, tiled=True, axis_index_groups=line_groups)
    signal = signal.reshape(ctx_size, tok_rows, channels)

    for at in range(1, freq_local):
        later = tie(spread[at : at + 1], [signal])
        spectra.append(lax.all_to_all(later[0], "ctx", 0, 0, tiled=True))

    if channels % 128 == 0:
        convolved = convolve_fused(signal, spectra, tables)
    else:
        spectrum = jnp.stack(spectra, 1).reshape(ctx_size * freq_local, 2, tok_rows, channels)
        convolved = convolve_plain(signal, spectrum)
    returned = lax.all_to_all(convolved, "ctx", 0, 0, tiled=True)
    return gate_output(returned, gate_q, plane, lines)


def solution(mesh):
    ctx_size = mesh.shape["ctx"]

    def whole(features, proj_weight, gate_q, gate_k, filter_spec):
        freq_local = filter_spec.shape[1] // ctx_size
        tables = [
            transform_tables(ctx_size, features.shape[0] // ctx_size, at, freq_local)
            for at in range(freq_local)
        ]
        return jax.shard_map(
            functools.partial(per_device, tables),
            mesh=mesh,
            in_specs=(
                P("ctx", "ch"),
                P("ctx", "ch"),
                P("ctx", "ch"),
                P("ctx", "ch"),
                P(None, "ctx", None, "ch"),
            ),
            out_specs=P("ctx", "ch"),
            check_vma=False,
        )(features, proj_weight, gate_q, gate_k, filter_spec)

    return whole
```

```python
import functools
import math

import jax
import jax.numpy as jnp
import numpy as np
from jax import lax
from jax.experimental import pallas as pl
from jax.experimental.pallas import tpu as pltpu
from jax.sharding import PartitionSpec as P

BF16 = jnp.bfloat16
F32 = jnp.float32
VMEM_LIMIT = 56 * 1024 * 1024
TIME_TILE = 16
FREQ_CHUNK = 4


def plane_size(ctx_size):
    size = 1
    while ctx_size % (2 * size) == 0 and 4 * size * size <= ctx_size:
        size *= 2
    return size


def best_scale(values):
    distinct, counts = np.unique(np.round(np.abs(values), 12), return_counts=True)
    best, best_error = 1.0, None
    for factor in np.linspace(1.0, 2.0, 2000, endpoint=False):
        scaled = distinct * factor
        rounded = scaled.astype(jnp.bfloat16).astype(np.float64)
        error = float((counts * (rounded - scaled) ** 2).sum()) / factor**2
        if best_error is None or error < best_error:
            best, best_error = float(factor), error
    return best


def split_table(table):
    high = table.astype(jnp.bfloat16)
    low = (table - high.astype(np.float64)).astype(jnp.bfloat16)
    return high, low


def transform_tables(slab_count, tok_rows, first, stride):
    freq_count = 2 * slab_count
    length = freq_count * tok_rows
    freq = np.arange(first, freq_count, stride)
    slab = np.arange(slab_count)
    fine = np.arange(TIME_TILE)
    group = np.arange(tok_rows // TIME_TILE)
    turns = (freq[:, None, None] * slab[None, None, :] % freq_count) / freq_count + (
        freq[:, None, None] * fine[None, :, None]
    ) / length
    phase = np.exp(-2j * np.pi * turns)
    slab_table = np.zeros((len(freq), 2, TIME_TILE, slab_count, TIME_TILE))
    for u in range(TIME_TILE):
        slab_table[:, 0, u, :, u] = phase[:, u].real
        slab_table[:, 1, u, :, u] = phase[:, u].imag
    slab_table = slab_table.reshape(len(freq) * 2 * TIME_TILE, slab_count * TIME_TILE)
    row = np.arange(tok_rows)
    turns = (row[:, None] * row[None, :] % tok_rows) / tok_rows
    cosine, sine = np.cos(2 * np.pi * turns), np.sin(2 * np.pi * turns)
    forward_rows = np.block([[cosine, sine], [-sine, cosine]])
    scale = best_scale(forward_rows)
    forward_rows = forward_rows * scale
    coarse = np.exp(-2j * np.pi * (freq[:, None] * TIME_TILE * group[None, :] % length) / length)
    coarse = np.stack([coarse.real, coarse.imag], axis=-1)
    inverse_scale = 1.0 / (length * scale * scale)
    return {
        "slab": split_table(slab_table),
        "slab_back": split_table(slab_table.T),
        "rows": forward_rows.astype(jnp.bfloat16),
        "rows_back": forward_rows.T.astype(jnp.bfloat16),
        "coarse": coarse.astype(np.float32).reshape(-1),
        "coarse_back": (coarse * inverse_scale).astype(np.float32).reshape(-1),
    }


def coarse_turn(ref, groups, freq, group):
    at = 2 * (freq * groups + group)
    return ref[at], ref[at + 1]


def slab_stage(coarse_ref, signal_ref, high_ref, low_ref, work_ref):
    slab_count, tok_rows, channels = signal_ref.shape
    freq_count = work_ref.shape[0]
    groups = tok_rows // TIME_TILE
    tile = TIME_TILE

    @pl.loop(0, groups // 2)
    def _(pair):
        parts = []
        for half in range(2):
            start = pl.multiple_of((2 * pair + half) * tile, tile)
            piece = signal_ref[:, pl.ds(start, tile), :]
            parts.append(piece.reshape(slab_count * tile, channels))
        block = jnp.concatenate(parts, axis=1)
        summed = jnp.dot(high_ref[...], block, preferred_element_type=F32)
        summed += jnp.dot(low_ref[...], block, preferred_element_type=F32)
        for freq in range(freq_count):
            base = freq * 2 * tile
            for half in range(2):
                lanes = slice(half * channels, (half + 1) * channels)
                real = summed[base : base + tile, lanes]
                imag = summed[base + tile : base + 2 * tile, lanes]
                cos, sin = coarse_turn(coarse_ref, groups, freq, 2 * pair + half)
                start = pl.multiple_of((2 * pair + half) * tile, tile)
                work_ref[freq, 0, pl.ds(start, tile), :] = (real * cos - imag * sin).astype(BF16)
                work_ref[freq, 1, pl.ds(start, tile), :] = (real * sin + imag * cos).astype(BF16)


def rows_stage(work_ref, rows_ref, first):
    _, _, tok_rows, channels = work_ref.shape
    wide = [work_ref[first + at].reshape(2 * tok_rows, channels) for at in range(FREQ_CHUNK)]
    return jnp.dot(rows_ref[...], jnp.concatenate(wide, axis=1), preferred_element_type=F32)


def product_and_back(forward, spectrum_ref, rows_back_ref, coarse_back_ref, work_ref, rest_ref, first):
    _, _, tok_rows, channels = work_ref.shape
    groups = tok_rows // TIME_TILE
    products = []
    for at in range(FREQ_CHUNK):
        real, imag = forward(at)
        spec_real = spectrum_ref[at, 0].astype(F32)
        spec_imag = spectrum_ref[at, 1].astype(F32)
        products.append(
            jnp.concatenate(
                [
                    (spec_real * real - spec_imag * imag).astype(BF16),
                    (spec_real * imag + spec_imag * real).astype(BF16),
                ],
                axis=0,
            )
        )
    inverse = jnp.dot(
        rows_back_ref[...], jnp.concatenate(products, axis=1), preferred_element_type=F32
    )
    for at in range(FREQ_CHUNK):
        lanes = slice(at * channels, (at + 1) * channels)
        for group in range(groups):
            rows = slice(group * TIME_TILE, (group + 1) * TIME_TILE)
            real = inverse[rows, lanes]
            imag = inverse[tok_rows + rows.start : tok_rows + rows.stop, lanes]
            cos, sin = coarse_turn(coarse_back_ref, groups, first + at, group)
            for part, value in enumerate((real * cos + imag * sin, imag * cos - real * sin)):
                high = value.astype(BF16)
                work_ref[first + at, part, rows, :] = high
                rest_ref[first + at, part, rows, :] = (value - high.astype(F32)).astype(BF16)


def slab_back_stage(work_ref, rest_ref, high_ref, low_ref, others, out_ref):
    slab_count, tok_rows, channels = out_ref.shape
    freq_count = work_ref.shape[0]
    tile = TIME_TILE
    depth = freq_count * 2 * tile

    @pl.loop(0, tok_rows // tile // 2)
    def _(pair):
        highs, lows = [], []
        for half in range(2):
            start = pl.multiple_of((2 * pair + half) * tile, tile)
            highs.append(work_ref[:, :, pl.ds(start, tile), :].reshape(depth, channels))
            lows.append(rest_ref[:, :, pl.ds(start, tile), :].reshape(depth, channels))
        high = jnp.concatenate(highs, axis=1)
        low = jnp.concatenate(lows, axis=1)
        total = jnp.dot(high_ref[...], high, preferred_element_type=F32)
        total += jnp.dot(low_ref[...], high, preferred_element_type=F32)
        total += jnp.dot(high_ref[...], low, preferred_element_type=F32)
        for half in range(2):
            start = pl.multiple_of((2 * pair + half) * tile, tile)
            lanes = slice(half * channels, (half + 1) * channels)
            value = total[:, lanes].reshape(slab_count, tile, channels)
            for other in others:
                value += other[:, pl.ds(start, tile), :]
            out_ref[:, pl.ds(start, tile), :] = value.astype(out_ref.dtype)


def convolve_kernel(
    coarse_ref,
    coarse_back_ref,
    signal_ref,
    spectrum_ref,
    slab_high_ref,
    slab_low_ref,
    back_high_ref,
    back_low_ref,
    rows_ref,
    rows_back_ref,
    out_ref,
    work_ref,
    rest_ref,
):
    _, tok_rows, channels = signal_ref.shape
    step = pl.program_id(0)

    @pl.when(step == 0)
    def _():
        slab_stage(coarse_ref, signal_ref, slab_high_ref, slab_low_ref, work_ref)

    first = step * FREQ_CHUNK
    transformed = rows_stage(work_ref, rows_ref, first)

    def forward(at):
        lanes = slice(at * channels, (at + 1) * channels)
        return transformed[:tok_rows, lanes], transformed[tok_rows:, lanes]

    product_and_back(forward, spectrum_ref, rows_back_ref, coarse_back_ref, work_ref, rest_ref, first)

    @pl.when(step == pl.num_programs(0) - 1)
    def _():
        slab_back_stage(work_ref, rest_ref, back_high_ref, back_low_ref, [], out_ref)


def forward_kernel(coarse_ref, signal_ref, slab_high_ref, slab_low_ref, rows_ref, out_ref, work_ref):
    _, tok_rows, channels = signal_ref.shape
    step = pl.program_id(0)

    @pl.when(step == 0)
    def _():
        slab_stage(coarse_ref, signal_ref, slab_high_ref, slab_low_ref, work_ref)

    transformed = rows_stage(work_ref, rows_ref, step * FREQ_CHUNK)
    for at in range(FREQ_CHUNK):
        lanes = slice(at * channels, (at + 1) * channels)
        out_ref[at, 0] = transformed[:tok_rows, lanes]
        out_ref[at, 1] = transformed[tok_rows:, lanes]


def inverse_kernel(
    coarse_back_ref,
    forward_ref,
    spectrum_ref,
    back_high_ref,
    back_low_ref,
    rows_back_ref,
    other_ref,
    out_ref,
    work_ref,
    rest_ref,
):
    step = pl.program_id(0)

    def forward(at):
        return forward_ref[at, 0], forward_ref[at, 1]

    product_and_back(
        forward, spectrum_ref, rows_back_ref, coarse_back_ref, work_ref, rest_ref, step * FREQ_CHUNK
    )

    @pl.when(step == pl.num_programs(0) - 1)
    def _():
        slab_back_stage(work_ref, rest_ref, back_high_ref, back_low_ref, [other_ref], out_ref)


def whole_block(array):
    return pl.BlockSpec(array.shape, lambda i: (0,) * array.ndim)


def frequency_call(kernel, name, freq_count, operands, out_shape, out_blocked, scratch, flops):
    arrays, specs = [], []

    def blocked(shape):
        return pl.BlockSpec((FREQ_CHUNK,) + shape[1:], lambda i: (i,) + (0,) * (len(shape) - 1))

    for array, kind in operands:
        array = jnp.asarray(array)
        arrays.append(array)
        if kind == "scalar":
            specs.append(pl.BlockSpec(memory_space=pltpu.SMEM))
        else:
            specs.append(blocked(array.shape) if kind == "blocked" else whole_block(array))
    moved = sum(a.size * a.dtype.itemsize for a in arrays)
    return pl.pallas_call(
        kernel,
        grid=(freq_count // FREQ_CHUNK,),
        in_specs=specs,
        out_specs=blocked(out_shape.shape) if out_blocked else whole_block(out_shape),
        out_shape=out_shape,
        scratch_shapes=scratch,
        compiler_params=pltpu.CompilerParams(
            dimension_semantics=("arbitrary",), vmem_limit_bytes=VMEM_LIMIT
        ),
        cost_estimate=pl.CostEstimate(flops=flops, bytes_accessed=moved, transcendentals=0),
        name=name,
    )(*arrays)


def convolve_fused(signal, spectra, tables):
    slab_count, tok_rows, channels = signal.shape
    freq_count = spectra[0].shape[0]
    rows_flops = 2 * freq_count * channels * (2 * tok_rows) ** 2
    slab_flops = 4 * freq_count * channels * tok_rows * slab_count * TIME_TILE
    work = pltpu.VMEM((freq_count, 2, tok_rows, channels), BF16)
    total = None
    for spectrum, table in zip(spectra[:-1], tables[:-1]):
        part = frequency_call(
            convolve_kernel,
            "convolve",
            freq_count,
            [
                (table["coarse"], "scalar"),
                (table["coarse_back"], "scalar"),
                (signal, "whole"),
                (spectrum, "blocked"),
                *[(t, "whole") for t in table["slab"]],
                *[(t, "whole") for t in table["slab_back"]],
                (table["rows"], "whole"),
                (table["rows_back"], "whole"),
            ],
            jax.ShapeDtypeStruct(signal.shape, F32),
            False,
            [work, work],
            2 * rows_flops + 5 * slab_flops,
        )
        total = part if total is None else total + part
    if total is None:
        total = jnp.zeros(signal.shape, F32)
    table = tables[-1]
    forward = frequency_call(
        forward_kernel,
        "forward",
        freq_count,
        [
            (table["coarse"], "scalar"),
            (signal, "whole"),
            *[(t, "whole") for t in table["slab"]],
            (table["rows"], "whole"),
        ],
        jax.ShapeDtypeStruct((freq_count, 2, tok_rows, channels), F32),
        True,
        [work],
        rows_flops + 2 * slab_flops,
    )
    return frequency_call(
        inverse_kernel,
        "inverse",
        freq_count,
        [
            (table["coarse_back"], "scalar"),
            (forward, "blocked"),
            (spectra[-1], "blocked"),
            *[(t, "whole") for t in table["slab_back"]],
            (table["rows_back"], "whole"),
            (total, "whole"),
        ],
        jax.ShapeDtypeStruct(signal.shape, BF16),
        False,
        [work, work],
        rows_flops + 3 * slab_flops,
    )


def spread_kernel(lines, channels, values_ref, out_ref):
    for line in range(lines):
        out_ref[line, 0, 0] = values_ref[0, 0, :, line * channels : (line + 1) * channels].astype(BF16)


def spread_spectrum(filter_spec, at, plane, lines):
    parts, _, tok_rows, group_channels = filter_spec.shape
    channels = group_channels // (plane * lines)
    if channels % 128:
        spec = filter_spec[:, at].reshape(parts, tok_rows, plane, lines, channels)
        spec = spec.transpose(3, 2, 0, 1, 4).astype(BF16)
    else:
        spec = pl.pallas_call(
            functools.partial(spread_kernel, lines, channels),
            grid=(parts, plane),
            in_specs=[
                pl.BlockSpec((1, 1, tok_rows, lines * channels), lambda i, j: (i, at, 0, j))
            ],
            out_specs=pl.BlockSpec((lines, 1, 1, tok_rows, channels), lambda i, j: (0, j, i, 0, 0)),
            out_shape=jax.ShapeDtypeStruct((lines, plane, parts, tok_rows, channels), BF16),
            compiler_params=pltpu.CompilerParams(
                dimension_semantics=("arbitrary", "arbitrary"), vmem_limit_bytes=VMEM_LIMIT
            ),
            cost_estimate=pl.CostEstimate(
                flops=0, bytes_accessed=6 * parts * tok_rows * group_channels, transcendentals=0
            ),
            name="spread_spectrum",
        )(filter_spec)
    return spec.reshape(plane * lines, parts, tok_rows, channels)


def gate_kernel(lines, channels, values_ref, gate_ref, out_ref):
    for line in range(lines):
        lanes = slice(line * channels, (line + 1) * channels)
        value = gate_ref[:, lanes].astype(F32) * values_ref[line, 0].astype(F32)
        out_ref[:, lanes] = value.astype(BF16)


def gate_output(returned, gate_q, plane, lines):
    _, tok_rows, channels = returned.shape
    returned = returned.reshape(lines, plane, tok_rows, channels)
    if channels % 128:
        returned = returned.transpose(2, 1, 0, 3).reshape(gate_q.shape)
        return (gate_q.astype(F32) * returned.astype(F32)).astype(BF16)
    flat = pl.BlockSpec((tok_rows, lines * channels), lambda i: (0, i))
    return pl.pallas_call(
        functools.partial(gate_kernel, lines, channels),
        grid=(plane,),
        in_specs=[pl.BlockSpec((lines, 1, tok_rows, channels), lambda i: (0, i, 0, 0)), flat],
        out_specs=flat,
        out_shape=jax.ShapeDtypeStruct(gate_q.shape, BF16),
        compiler_params=pltpu.CompilerParams(
            dimension_semantics=("arbitrary",), vmem_limit_bytes=VMEM_LIMIT
        ),
        cost_estimate=pl.CostEstimate(
            flops=gate_q.size, bytes_accessed=6 * gate_q.size, transcendentals=0
        ),
        name="gate_output",
    )(returned, gate_q)


def convolve_plain(signal, spectrum):
    slab_count, tok_rows, channels = signal.shape
    freq_count = 2 * slab_count
    length = freq_count * tok_rows

    def phase(left, right, modulus):
        turns = (left[:, None] * right[None, :] % modulus).astype(F32) * (2.0 * math.pi / modulus)
        return jnp.cos(turns), jnp.sin(turns)

    dot = functools.partial(jnp.einsum, precision=lax.Precision.HIGH, preferred_element_type=F32)
    freq = jnp.arange(freq_count, dtype=jnp.int32)
    slab = jnp.arange(slab_count, dtype=jnp.int32)
    row = jnp.arange(tok_rows, dtype=jnp.int32)
    slab_cos, slab_sin = phase(freq, slab, freq_count)
    turn_cos, turn_sin = (part[:, :, None] for part in phase(freq, row, length))
    row_cos, row_sin = phase(row, row, tok_rows)
    values = signal.astype(F32)
    real, imag = dot("ks,stc->ktc", slab_cos, values), -dot("ks,stc->ktc", slab_sin, values)
    real, imag = real * turn_cos + imag * turn_sin, imag * turn_cos - real * turn_sin
    real, imag = (
        dot("jt,ktc->kjc", row_cos, real) + dot("jt,ktc->kjc", row_sin, imag),
        dot("jt,ktc->kjc", row_cos, imag) - dot("jt,ktc->kjc", row_sin, real),
    )
    spec_real, spec_imag = spectrum[:, 0].astype(F32), spectrum[:, 1].astype(F32)
    real, imag = real * spec_real - imag * spec_imag, imag * spec_real + real * spec_imag
    real, imag = (
        dot("jt,ktc->kjc", row_cos, real) - dot("jt,ktc->kjc", row_sin, imag),
        dot("jt,ktc->kjc", row_cos, imag) + dot("jt,ktc->kjc", row_sin, real),
    )
    real, imag = real * turn_cos - imag * turn_sin, imag * turn_cos + real * turn_sin
    values = dot("ks,ktc->stc", slab_cos, real) - dot("ks,ktc->stc", slab_sin, imag)
    return (values / length).astype(BF16)


def project_kernel(lines, plane, place_ref, *refs):
    along_refs, refs = refs[:lines], refs[lines:]
    feature_refs, refs = refs[: 4 * plane], refs[4 * plane :]
    gate_refs, (out_ref, weight_ref) = refs[:plane], refs[plane:]
    line_at, plane_at, core = place_ref[0], place_ref[1], place_ref[2]
    for k in range(lines):
        line = lax.rem(line_at + lines - k, lines)
        weight_ref[pl.ds(line * plane, plane)] = along_refs[k][...]
    _, weight_rows, wide = weight_ref.shape
    depth = feature_refs[0].shape[1]
    channels = out_ref.shape[3]
    blocks = depth // weight_rows
    for d in range(plane):
        total = None
        for e in range(2):
            for half in range(2):
                first = (2 * lax.rem(core + e, 2) + half) * blocks
                weights = weight_ref[pl.ds(first, blocks)].reshape(depth, wide)
                features = feature_refs[(e * plane + d) * 2 + half][...]
                term = jnp.dot(features, weights, preferred_element_type=F32)
                total = term if total is None else total + term
        value = (gate_refs[d][...].astype(F32) * total).astype(BF16)
        for line in range(lines):
            out_ref[line, plane_at ^ d] = value[:, line * channels : (line + 1) * channels]


def project_fused(place, along, pieces, gates):
    lines, plane = len(along), len(gates)
    _, weight_rows, wide = along[0].shape
    tok_rows = gates[0].shape[0]
    flat = [half for core in pieces for d in core for half in d]
    operands = [*along, *flat, *gates]
    local = pl.BlockSpec(memory_space=pltpu.VMEM)
    return pl.pallas_call(
        functools.partial(project_kernel, lines, plane),
        in_specs=[pl.BlockSpec(memory_space=pltpu.SMEM)] + [local] * len(operands),
        out_specs=local,
        out_shape=jax.ShapeDtypeStruct((lines, plane, tok_rows, wide // lines), BF16),
        scratch_shapes=[pltpu.VMEM((lines * plane, weight_rows, wide), BF16)],
        compiler_params=pltpu.CompilerParams(vmem_limit_bytes=VMEM_LIMIT),
        cost_estimate=pl.CostEstimate(
            flops=2 * wide * sum(f.size for f in flat),
            bytes_accessed=2 * sum(o.size for o in operands),
            transcendentals=0,
        ),
        name="project",
    )(place, *operands)


def project_plain(place, along, pieces, gates):
    line_at, plane_at, core = place[0], place[1], place[2]
    lines = len(along)
    pieces = [jnp.stack([jnp.stack(d) for d in by_core]) for by_core in pieces]
    gates = jnp.stack(gates)
    plane, _, tok_rows, depth = pieces[0].shape
    wide = along[0].shape[2]
    take_line = jnp.mod(line_at - jnp.arange(lines), lines)
    take_plane = jnp.arange(plane) ^ plane_at
    weight = jnp.stack(along)[take_line].reshape(len(pieces), 2, depth, wide)
    total = jnp.zeros((plane, tok_rows, wide), F32)
    for e, piece in enumerate(pieces):
        at = jnp.mod(core - e, len(pieces))
        total += jnp.einsum("phtk,hkc->ptc", piece, weight[at], preferred_element_type=F32)
    value = (gates.astype(F32) * total).astype(BF16)[take_plane]
    return value.reshape(plane, tok_rows, lines, wide // lines).transpose(2, 0, 1, 3)


def after(values, earlier):
    values, earlier = list(values), list(earlier)
    if not earlier:
        return values
    anywhere = pl.BlockSpec(memory_space=pl.ANY)
    return pl.pallas_call(
        lambda *refs: None,
        in_specs=[anywhere] * (len(values) + len(earlier)),
        out_specs=[anywhere] * len(values),
        out_shape=[jax.ShapeDtypeStruct(v.shape, v.dtype) for v in values],
        input_output_aliases={i: i for i in range(len(values))},
        cost_estimate=pl.CostEstimate(flops=0, bytes_accessed=0, transcendentals=0),
        name="after",
    )(*values, *earlier)


def per_device(tables, features, proj_weight, gate_q, gate_k, filter_spec):
    ctx_size = lax.axis_size("ctx")
    ch_size = lax.axis_size("ch")
    plane = plane_size(ctx_size)
    lines = ctx_size // plane
    me = lax.axis_index("ctx")
    ch_me = lax.axis_index("ch")
    line_at, plane_at = me // plane, me % plane
    tok_rows, feat_cols = features.shape
    weight_rows, group_channels = proj_weight.shape
    wide = group_channels // plane
    channels = wide // lines
    freq_local = filter_spec.shape[1]
    tie = after if channels % 128 == 0 else lambda values, earlier: values

    plane_groups = [[z * plane + p for p in range(plane)] for z in range(lines)]
    line_groups = [[z * plane + p for z in range(lines)] for p in range(plane)]
    onward = [(i, (i + plane) % ctx_size) for i in range(ctx_size)]

    def swap(value, d):
        perm = [(i, i // plane * plane + (i % plane ^ d)) for i in range(ctx_size)]
        return lax.ppermute(value, "ctx", perm)

    def other_core(value, e):
        return lax.ppermute(value, "ch", [(i, (i + e) % ch_size) for i in range(ch_size)])

    weight = proj_weight.reshape(weight_rows, plane, wide).transpose(1, 0, 2)
    weight = lax.all_to_all(weight, "ctx", 0, 0, tiled=True, axis_index_groups=plane_groups)
    along = [weight]

    halves = jnp.split(features, 2, axis=1)
    held = [{0: half} for half in halves]
    arrival = [[0], [0]]
    bits = [1 << b for b in range(plane.bit_length() - 1)]
    rounds = [
        (turn, k) for turn in range(len(bits)) for k in reversed(range(1 << turn))
    ]

    def feature_round(turn, k, beside):
        ds = [bits[(turn + at) % len(bits)] for at in range(2)]
        sources = [arrival[at][k] for at in range(2)]
        values = [held[at][sources[at]] for at in range(2)]
        if sources[0]:
            values = tie(values, beside)
        new = []
        for at in range(2):
            held[at][sources[at]] = values[at]
            place = sources[at] ^ ds[at]
            held[at][place] = swap(values[at], ds[at])
            new.append(held[at][place])
        if k == 0:
            arrival[:] = [sorted(held[at], key=list(held[at]).index) for at in range(2)]
        return new

    gate_blocks = gate_k.reshape(tok_rows, plane, wide)
    gates = [
        lax.dynamic_index_in_dim(gate_blocks, plane_at ^ d, 1, keepdims=False) for d in range(plane)
    ]
    spread = [spread_spectrum(filter_spec, at, plane, lines) for at in range(freq_local)]
    beside = []
    for step in range(max(lines - 1, len(rounds))):
        if step < lines - 1:
            along[-1] = tie(along[-1:], beside)[0]
            along.append(lax.ppermute(along[-1], "ctx", onward))
        if step < len(rounds):
            beside = feature_round(*rounds[step], beside + along[step : step + 1])
        beside = beside + spread[step : step + 1] + (gates if step == 1 else [])
    gates = tie(gates, along[-1:])
    gates = [swap(gate, d) if d else gate for d, gate in enumerate(gates)]

    first = tie(spread[:1], along[-1:] + beside)
    spectra = [lax.all_to_all(first[0], "ctx", 0, 0, tiled=True)]

    place = jnp.stack([line_at, plane_at, ch_me]).astype(jnp.int32)
    own = [[held[at][d] for at in range(2)] for d in range(plane)]
    pieces = [own] + [
        [[other_core(half, e) for half in d] for d in own] for e in range(1, ch_size)
    ]
    fits = channels % 128 == 0 and ch_size == 2 and feat_cols // 2 % weight_rows == 0
    if fits and weight_rows % 16 == 0 and tok_rows % 16 == 0:
        signal = project_fused(place, along, pieces, gates)
    else:
        signal = project_plain(place, along, pieces, gates)
    signal = tie([signal], spectra)[0]
    signal = lax.all_to_all(signal, "ctx", 0, 0, tiled=True, axis_index_groups=line_groups)
    signal = signal.reshape(ctx_size, tok_rows, channels)

    for at in range(1, freq_local):
        later = tie(spread[at : at + 1], [signal])
        spectra.append(lax.all_to_all(later[0], "ctx", 0, 0, tiled=True))

    if channels % 128 == 0:
        convolved = convolve_fused(signal, spectra, tables)
    else:
        spectrum = jnp.stack(spectra, 1).reshape(ctx_size * freq_local, 2, tok_rows, channels)
        convolved = convolve_plain(signal, spectrum)
    returned = lax.all_to_all(convolved, "ctx", 0, 0, tiled=True)
    return gate_output(returned, gate_q, plane, lines)


def solution(mesh):
    ctx_size = mesh.shape["ctx"]

    def whole(features, proj_weight, gate_q, gate_k, filter_spec):
        freq_local = filter_spec.shape[1] // ctx_size
        tables = [
            transform_tables(ctx_size, features.shape[0] // ctx_size, at, freq_local)
            for at in range(freq_local)
        ]
        return jax.shard_map(
            functools.partial(per_device, tables),
            mesh=mesh,
            in_specs=(
                P("ctx", "ch"),
                P("ctx", "ch"),
                P("ctx", "ch"),
                P("ctx", "ch"),
                P(None, "ctx", None, "ch"),
            ),
            out_specs=P("ctx", "ch"),
            check_vma=False,
        )(features, proj_weight, gate_q, gate_k, filter_spec)

    return whole
```

```python
import functools
import math

import jax
import jax.numpy as jnp
import numpy as np
from jax import lax
from jax.experimental import pallas as pl
from jax.experimental.pallas import tpu as pltpu
from jax.sharding import PartitionSpec as P

BF16 = jnp.bfloat16
F32 = jnp.float32
VMEM_LIMIT = 56 * 1024 * 1024
TIME_TILE = 16
FREQ_CHUNK = 4
PRODUCT_CHUNK = 2


def plane_size(ctx_size):
    size = 1
    while ctx_size % (2 * size) == 0 and 4 * size * size <= ctx_size:
        size *= 2
    return size


def best_scale(values):
    distinct, counts = np.unique(np.round(np.abs(values), 12), return_counts=True)
    best, best_error = 1.0, None
    for factor in np.linspace(1.0, 2.0, 2000, endpoint=False):
        scaled = distinct * factor
        rounded = scaled.astype(jnp.bfloat16).astype(np.float64)
        error = float((counts * (rounded - scaled) ** 2).sum()) / factor**2
        if best_error is None or error < best_error:
            best, best_error = float(factor), error
    return best


def split_table(table):
    high = table.astype(jnp.bfloat16)
    low = (table - high.astype(np.float64)).astype(jnp.bfloat16)
    return high, low


def transform_tables(slab_count, tok_rows, first, stride):
    freq_count = 2 * slab_count
    length = freq_count * tok_rows
    freq = np.arange(first, freq_count, stride)
    slab = np.arange(slab_count)
    fine = np.arange(TIME_TILE)
    group = np.arange(tok_rows // TIME_TILE)
    turns = (freq[:, None, None] * slab[None, None, :] % freq_count) / freq_count + (
        freq[:, None, None] * fine[None, :, None]
    ) / length
    phase = np.exp(-2j * np.pi * turns)
    slab_table = np.zeros((len(freq), 2, TIME_TILE, slab_count, TIME_TILE))
    for u in range(TIME_TILE):
        slab_table[:, 0, u, :, u] = phase[:, u].real
        slab_table[:, 1, u, :, u] = phase[:, u].imag
    slab_table = slab_table.reshape(len(freq) * 2 * TIME_TILE, slab_count * TIME_TILE)
    row = np.arange(tok_rows)
    turns = (row[:, None] * row[None, :] % tok_rows) / tok_rows
    cosine, sine = np.cos(2 * np.pi * turns), np.sin(2 * np.pi * turns)
    forward_rows = np.block([[cosine, sine], [-sine, cosine]])
    scale = best_scale(forward_rows)
    forward_rows = forward_rows * scale
    coarse = np.exp(-2j * np.pi * (freq[:, None] * TIME_TILE * group[None, :] % length) / length)
    coarse = np.stack([coarse.real, coarse.imag], axis=-1)
    inverse_scale = 1.0 / (length * scale * scale)
    return {
        "slab": split_table(slab_table),
        "slab_back": split_table(slab_table.T),
        "rows": forward_rows.astype(jnp.bfloat16),
        "rows_back": forward_rows.T.astype(jnp.bfloat16),
        "coarse": coarse.astype(np.float32).reshape(-1),
        "coarse_back": (coarse * inverse_scale).astype(np.float32).reshape(-1),
    }


def coarse_turn(ref, groups, freq, group):
    at = 2 * (freq * groups + group)
    return ref[at], ref[at + 1]


def slab_stage(coarse_ref, signal_ref, high_ref, low_ref, work_ref):
    slab_count, tok_rows, channels = signal_ref.shape
    freq_count = work_ref.shape[0]
    groups = tok_rows // TIME_TILE
    tile = TIME_TILE

    @pl.loop(0, groups // 2)
    def _(pair):
        parts = []
        for half in range(2):
            start = pl.multiple_of((2 * pair + half) * tile, tile)
            piece = signal_ref[:, pl.ds(start, tile), :]
            parts.append(piece.reshape(slab_count * tile, channels))
        block = jnp.concatenate(parts, axis=1)
        summed = jnp.dot(high_ref[...], block, preferred_element_type=F32)
        summed += jnp.dot(low_ref[...], block, preferred_element_type=F32)
        for freq in range(freq_count):
            base = freq * 2 * tile
            for half in range(2):
                lanes = slice(half * channels, (half + 1) * channels)
                real = summed[base : base + tile, lanes]
                imag = summed[base + tile : base + 2 * tile, lanes]
                cos, sin = coarse_turn(coarse_ref, groups, freq, 2 * pair + half)
                start = pl.multiple_of((2 * pair + half) * tile, tile)
                work_ref[freq, 0, pl.ds(start, tile), :] = (real * cos - imag * sin).astype(BF16)
                work_ref[freq, 1, pl.ds(start, tile), :] = (real * sin + imag * cos).astype(BF16)


def rows_stage(work_ref, rows_ref, first):
    _, _, tok_rows, channels = work_ref.shape
    wide = [work_ref[first + at].reshape(2 * tok_rows, channels) for at in range(FREQ_CHUNK)]
    return jnp.dot(rows_ref[...], jnp.concatenate(wide, axis=1), preferred_element_type=F32)


def product_and_back(forward, spectrum_ref, rows_back_ref, coarse_back_ref, work_ref, rest_ref, first):
    _, _, tok_rows, channels = work_ref.shape
    groups = tok_rows // TIME_TILE
    for chunk in range(0, FREQ_CHUNK, PRODUCT_CHUNK):
        products = []
        for at in range(chunk, chunk + PRODUCT_CHUNK):
            real, imag = forward(at)
            spec_real = spectrum_ref[at, 0].astype(F32)
            spec_imag = spectrum_ref[at, 1].astype(F32)
            products.append(
                jnp.concatenate(
                    [
                        (spec_real * real - spec_imag * imag).astype(BF16),
                        (spec_real * imag + spec_imag * real).astype(BF16),
                    ],
                    axis=0,
                )
            )
        inverse = jnp.dot(
            rows_back_ref[...], jnp.concatenate(products, axis=1), preferred_element_type=F32
        )
        for at in range(chunk, chunk + PRODUCT_CHUNK):
            lanes = slice((at - chunk) * channels, (at - chunk + 1) * channels)
            for group in range(groups):
                rows = slice(group * TIME_TILE, (group + 1) * TIME_TILE)
                real = inverse[rows, lanes]
                imag = inverse[tok_rows + rows.start : tok_rows + rows.stop, lanes]
                cos, sin = coarse_turn(coarse_back_ref, groups, first + at, group)
                for part, value in enumerate((real * cos + imag * sin, imag * cos - real * sin)):
                    high = value.astype(BF16)
                    work_ref[first + at, part, rows, :] = high
                    rest_ref[first + at, part, rows, :] = (value - high.astype(F32)).astype(BF16)


def slab_back_stage(work_ref, rest_ref, high_ref, low_ref, others, out_ref):
    slab_count, tok_rows, channels = out_ref.shape
    freq_count = work_ref.shape[0]
    tile = TIME_TILE
    depth = freq_count * 2 * tile

    @pl.loop(0, tok_rows // tile // 2)
    def _(pair):
        highs, lows = [], []
        for half in range(2):
            start = pl.multiple_of((2 * pair + half) * tile, tile)
            highs.append(work_ref[:, :, pl.ds(start, tile), :].reshape(depth, channels))
            lows.append(rest_ref[:, :, pl.ds(start, tile), :].reshape(depth, channels))
        high = jnp.concatenate(highs, axis=1)
        low = jnp.concatenate(lows, axis=1)
        total = jnp.dot(high_ref[...], high, preferred_element_type=F32)
        total += jnp.dot(low_ref[...], high, preferred_element_type=F32)
        total += jnp.dot(high_ref[...], low, preferred_element_type=F32)
        for half in range(2):
            start = pl.multiple_of((2 * pair + half) * tile, tile)
            lanes = slice(half * channels, (half + 1) * channels)
            value = total[:, lanes].reshape(slab_count, tile, channels)
            for other in others:
                value += other[:, pl.ds(start, tile), :]
            out_ref[:, pl.ds(start, tile), :] = value.astype(out_ref.dtype)


def gather_signal(place_ref, piece_refs, signal_ref):
    lines = len(piece_refs)
    for k, ref in enumerate(piece_refs):
        line = lax.rem(place_ref[0] + lines - k, lines)
        signal_ref[pl.ds(line * ref.shape[0], ref.shape[0])] = ref[...]


def convolve_kernel(lines, place_ref, coarse_ref, coarse_back_ref, *refs):
    piece_refs, refs = refs[:lines], refs[lines:]
    spectrum_ref, slab_high_ref, slab_low_ref, back_high_ref, back_low_ref = refs[:5]
    rows_ref, rows_back_ref, out_ref, signal_ref, work_ref, rest_ref = refs[5:]
    _, tok_rows, channels = signal_ref.shape
    step = pl.program_id(0)

    @pl.when(step == 0)
    def _():
        gather_signal(place_ref, piece_refs, signal_ref)
        slab_stage(coarse_ref, signal_ref, slab_high_ref, slab_low_ref, work_ref)

    first = step * FREQ_CHUNK
    transformed = rows_stage(work_ref, rows_ref, first)

    def forward(at):
        lanes = slice(at * channels, (at + 1) * channels)
        return transformed[:tok_rows, lanes], transformed[tok_rows:, lanes]

    product_and_back(forward, spectrum_ref, rows_back_ref, coarse_back_ref, work_ref, rest_ref, first)

    @pl.when(step == pl.num_programs(0) - 1)
    def _():
        slab_back_stage(work_ref, rest_ref, back_high_ref, back_low_ref, [], out_ref)


def forward_kernel(lines, place_ref, coarse_ref, *refs):
    piece_refs, refs = refs[:lines], refs[lines:]
    slab_high_ref, slab_low_ref, rows_ref, out_ref, signal_ref, work_ref = refs
    _, tok_rows, channels = signal_ref.shape
    step = pl.program_id(0)

    @pl.when(step == 0)
    def _():
        gather_signal(place_ref, piece_refs, signal_ref)
        slab_stage(coarse_ref, signal_ref, slab_high_ref, slab_low_ref, work_ref)

    transformed = rows_stage(work_ref, rows_ref, step * FREQ_CHUNK)
    for at in range(FREQ_CHUNK):
        lanes = slice(at * channels, (at + 1) * channels)
        out_ref[at, 0] = transformed[:tok_rows, lanes]
        out_ref[at, 1] = transformed[tok_rows:, lanes]


def inverse_kernel(
    coarse_back_ref,
    forward_ref,
    spectrum_ref,
    back_high_ref,
    back_low_ref,
    rows_back_ref,
    other_ref,
    out_ref,
    work_ref,
    rest_ref,
):
    step = pl.program_id(0)

    def forward(at):
        return forward_ref[at, 0], forward_ref[at, 1]

    product_and_back(
        forward, spectrum_ref, rows_back_ref, coarse_back_ref, work_ref, rest_ref, step * FREQ_CHUNK
    )

    @pl.when(step == pl.num_programs(0) - 1)
    def _():
        slab_back_stage(work_ref, rest_ref, back_high_ref, back_low_ref, [other_ref], out_ref)


def whole_block(array):
    return pl.BlockSpec(array.shape, lambda i: (0,) * array.ndim)


def frequency_call(kernel, name, freq_count, operands, out_shape, out_blocked, scratch, flops):
    arrays, specs = [], []

    def blocked(shape):
        return pl.BlockSpec((FREQ_CHUNK,) + shape[1:], lambda i: (i,) + (0,) * (len(shape) - 1))

    for array, kind in operands:
        array = jnp.asarray(array)
        arrays.append(array)
        if kind == "scalar":
            specs.append(pl.BlockSpec(memory_space=pltpu.SMEM))
        else:
            specs.append(blocked(array.shape) if kind == "blocked" else whole_block(array))
    moved = sum(a.size * a.dtype.itemsize for a in arrays)
    return pl.pallas_call(
        kernel,
        grid=(freq_count // FREQ_CHUNK,),
        in_specs=specs,
        out_specs=blocked(out_shape.shape) if out_blocked else whole_block(out_shape),
        out_shape=out_shape,
        scratch_shapes=scratch,
        compiler_params=pltpu.CompilerParams(
            dimension_semantics=("arbitrary",), vmem_limit_bytes=VMEM_LIMIT
        ),
        cost_estimate=pl.CostEstimate(flops=flops, bytes_accessed=moved, transcendentals=0),
        name=name,
    )(*arrays)


def convolve_fused(place, pieces, spectra, tables):
    lines = len(pieces)
    plane, tok_rows, channels = pieces[0].shape
    slab_count = lines * plane
    signal = jax.ShapeDtypeStruct((slab_count, tok_rows, channels), BF16)
    gathered = pltpu.VMEM(signal.shape, BF16)
    freq_count = spectra[0].shape[0]
    rows_flops = 2 * freq_count * channels * (2 * tok_rows) ** 2
    slab_flops = 4 * freq_count * channels * tok_rows * slab_count * TIME_TILE
    work = pltpu.VMEM((freq_count, 2, tok_rows, channels), BF16)
    total = None
    for spectrum, table in zip(spectra[:-1], tables[:-1]):
        part = frequency_call(
            functools.partial(convolve_kernel, lines),
            "convolve",
            freq_count,
            [
                (place, "scalar"),
                (table["coarse"], "scalar"),
                (table["coarse_back"], "scalar"),
                *[(piece, "whole") for piece in pieces],
                (spectrum, "blocked"),
                *[(t, "whole") for t in table["slab"]],
                *[(t, "whole") for t in table["slab_back"]],
                (table["rows"], "whole"),
                (table["rows_back"], "whole"),
            ],
            jax.ShapeDtypeStruct(signal.shape, F32),
            False,
            [gathered, work, work],
            2 * rows_flops + 5 * slab_flops,
        )
        total = part if total is None else total + part
    if total is None:
        total = jnp.zeros(signal.shape, F32)
    table = tables[-1]
    forward = frequency_call(
        functools.partial(forward_kernel, lines),
        "forward",
        freq_count,
        [
            (place, "scalar"),
            (table["coarse"], "scalar"),
            *[(piece, "whole") for piece in pieces],
            *[(t, "whole") for t in table["slab"]],
            (table["rows"], "whole"),
        ],
        jax.ShapeDtypeStruct((freq_count, 2, tok_rows, channels), F32),
        True,
        [gathered, work],
        rows_flops + 2 * slab_flops,
    )
    return frequency_call(
        inverse_kernel,
        "inverse",
        freq_count,
        [
            (table["coarse_back"], "scalar"),
            (forward, "blocked"),
            (spectra[-1], "blocked"),
            *[(t, "whole") for t in table["slab_back"]],
            (table["rows_back"], "whole"),
            (total, "whole"),
        ],
        jax.ShapeDtypeStruct(signal.shape, BF16),
        False,
        [work, work],
        rows_flops + 3 * slab_flops,
    )


def spread_kernel(lines, channels, values_ref, out_ref):
    for line in range(lines):
        out_ref[line, 0, 0] = values_ref[0, 0, :, line * channels : (line + 1) * channels].astype(BF16)


def spread_spectrum(filter_spec, at, plane, lines):
    parts, _, tok_rows, group_channels = filter_spec.shape
    channels = group_channels // (plane * lines)
    if channels % 128:
        spec = filter_spec[:, at].reshape(parts, tok_rows, plane, lines, channels)
        spec = spec.transpose(3, 2, 0, 1, 4).astype(BF16)
    else:
        spec = pl.pallas_call(
            functools.partial(spread_kernel, lines, channels),
            grid=(parts, plane),
            in_specs=[
                pl.BlockSpec((1, 1, tok_rows, lines * channels), lambda i, j: (i, at, 0, j))
            ],
            out_specs=pl.BlockSpec((lines, 1, 1, tok_rows, channels), lambda i, j: (0, j, i, 0, 0)),
            out_shape=jax.ShapeDtypeStruct((lines, plane, parts, tok_rows, channels), BF16),
            compiler_params=pltpu.CompilerParams(
                dimension_semantics=("arbitrary", "arbitrary"), vmem_limit_bytes=VMEM_LIMIT
            ),
            cost_estimate=pl.CostEstimate(
                flops=0, bytes_accessed=6 * parts * tok_rows * group_channels, transcendentals=0
            ),
            name="spread_spectrum",
        )(filter_spec)
    return spec.reshape(plane * lines, parts, tok_rows, channels)


def gate_kernel(lines, channels, values_ref, gate_ref, out_ref):
    for line in range(lines):
        lanes = slice(line * channels, (line + 1) * channels)
        value = gate_ref[:, lanes].astype(F32) * values_ref[line, 0].astype(F32)
        out_ref[:, lanes] = value.astype(BF16)


def gate_output(returned, gate_q, plane, lines):
    _, tok_rows, channels = returned.shape
    returned = returned.reshape(lines, plane, tok_rows, channels)
    if channels % 128:
        returned = returned.transpose(2, 1, 0, 3).reshape(gate_q.shape)
        return (gate_q.astype(F32) * returned.astype(F32)).astype(BF16)
    flat = pl.BlockSpec((tok_rows, lines * channels), lambda i: (0, i))
    return pl.pallas_call(
        functools.partial(gate_kernel, lines, channels),
        grid=(plane,),
        in_specs=[pl.BlockSpec((lines, 1, tok_rows, channels), lambda i: (0, i, 0, 0)), flat],
        out_specs=flat,
        out_shape=jax.ShapeDtypeStruct(gate_q.shape, BF16),
        compiler_params=pltpu.CompilerParams(
            dimension_semantics=("arbitrary",), vmem_limit_bytes=VMEM_LIMIT
        ),
        cost_estimate=pl.CostEstimate(
            flops=gate_q.size, bytes_accessed=6 * gate_q.size, transcendentals=0
        ),
        name="gate_output",
    )(returned, gate_q)


def convolve_plain(signal, spectrum):
    slab_count, tok_rows, channels = signal.shape
    freq_count = 2 * slab_count
    length = freq_count * tok_rows

    def phase(left, right, modulus):
        turns = (left[:, None] * right[None, :] % modulus).astype(F32) * (2.0 * math.pi / modulus)
        return jnp.cos(turns), jnp.sin(turns)

    dot = functools.partial(jnp.einsum, precision=lax.Precision.HIGH, preferred_element_type=F32)
    freq = jnp.arange(freq_count, dtype=jnp.int32)
    slab = jnp.arange(slab_count, dtype=jnp.int32)
    row = jnp.arange(tok_rows, dtype=jnp.int32)
    slab_cos, slab_sin = phase(freq, slab, freq_count)
    turn_cos, turn_sin = (part[:, :, None] for part in phase(freq, row, length))
    row_cos, row_sin = phase(row, row, tok_rows)
    values = signal.astype(F32)
    real, imag = dot("ks,stc->ktc", slab_cos, values), -dot("ks,stc->ktc", slab_sin, values)
    real, imag = real * turn_cos + imag * turn_sin, imag * turn_cos - real * turn_sin
    real, imag = (
        dot("jt,ktc->kjc", row_cos, real) + dot("jt,ktc->kjc", row_sin, imag),
        dot("jt,ktc->kjc", row_cos, imag) - dot("jt,ktc->kjc", row_sin, real),
    )
    spec_real, spec_imag = spectrum[:, 0].astype(F32), spectrum[:, 1].astype(F32)
    real, imag = real * spec_real - imag * spec_imag, imag * spec_real + real * spec_imag
    real, imag = (
        dot("jt,ktc->kjc", row_cos, real) - dot("jt,ktc->kjc", row_sin, imag),
        dot("jt,ktc->kjc", row_cos, imag) + dot("jt,ktc->kjc", row_sin, real),
    )
    real, imag = real * turn_cos - imag * turn_sin, imag * turn_cos + real * turn_sin
    values = dot("ks,ktc->stc", slab_cos, real) - dot("ks,ktc->stc", slab_sin, imag)
    return (values / length).astype(BF16)


def project_kernel(lines, plane, place_ref, *refs):
    along_refs, refs = refs[:lines], refs[lines:]
    feature_refs, refs = refs[: 4 * plane], refs[4 * plane :]
    gate_refs, (out_ref, weight_ref) = refs[:plane], refs[plane:]
    line_at, plane_at, core = place_ref[0], place_ref[1], place_ref[2]
    for k in range(lines):
        line = lax.rem(line_at + lines - k, lines)
        weight_ref[pl.ds(line * plane, plane)] = along_refs[k][...]
    _, weight_rows, wide = weight_ref.shape
    depth = feature_refs[0].shape[1]
    channels = out_ref.shape[3]
    blocks = depth // weight_rows
    for d in range(plane):
        total = None
        for e in range(2):
            for half in range(2):
                first = (2 * lax.rem(core + e, 2) + half) * blocks
                weights = weight_ref[pl.ds(first, blocks)].reshape(depth, wide)
                features = feature_refs[(e * plane + d) * 2 + half][...]
                term = jnp.dot(features, weights, preferred_element_type=F32)
                total = term if total is None else total + term
        value = (gate_refs[d][...].astype(F32) * total).astype(BF16)
        for line in range(lines):
            onward = lax.rem(line + lines - line_at, lines)
            out_ref[onward, plane_at ^ d] = value[:, line * channels : (line + 1) * channels]


def project_fused(place, along, pieces, gates):
    lines, plane = len(along), len(gates)
    _, weight_rows, wide = along[0].shape
    tok_rows = gates[0].shape[0]
    flat = [half for core in pieces for d in core for half in d]
    operands = [*along, *flat, *gates]
    local = pl.BlockSpec(memory_space=pltpu.VMEM)
    return pl.pallas_call(
        functools.partial(project_kernel, lines, plane),
        in_specs=[pl.BlockSpec(memory_space=pltpu.SMEM)] + [local] * len(operands),
        out_specs=local,
        out_shape=jax.ShapeDtypeStruct((lines, plane, tok_rows, wide // lines), BF16),
        scratch_shapes=[pltpu.VMEM((lines * plane, weight_rows, wide), BF16)],
        compiler_params=pltpu.CompilerParams(vmem_limit_bytes=VMEM_LIMIT),
        cost_estimate=pl.CostEstimate(
            flops=2 * wide * sum(f.size for f in flat),
            bytes_accessed=2 * sum(o.size for o in operands),
            transcendentals=0,
        ),
        name="project",
    )(place, *operands)


def project_plain(place, along, pieces, gates):
    line_at, plane_at, core = place[0], place[1], place[2]
    lines = len(along)
    pieces = [jnp.stack([jnp.stack(d) for d in by_core]) for by_core in pieces]
    gates = jnp.stack(gates)
    plane, _, tok_rows, depth = pieces[0].shape
    wide = along[0].shape[2]
    take_line = jnp.mod(line_at - jnp.arange(lines), lines)
    take_plane = jnp.arange(plane) ^ plane_at
    weight = jnp.stack(along)[take_line].reshape(len(pieces), 2, depth, wide)
    total = jnp.zeros((plane, tok_rows, wide), F32)
    for e, piece in enumerate(pieces):
        at = jnp.mod(core - e, len(pieces))
        total += jnp.einsum("phtk,hkc->ptc", piece, weight[at], preferred_element_type=F32)
    value = (gates.astype(F32) * total).astype(BF16)[take_plane]
    value = value.reshape(plane, tok_rows, lines, wide // lines).transpose(2, 0, 1, 3)
    return value[jnp.mod(line_at + jnp.arange(lines), lines)]


def after(values, earlier):
    values, earlier = list(values), list(earlier)
    if not earlier:
        return values
    anywhere = pl.BlockSpec(memory_space=pl.ANY)
    return pl.pallas_call(
        lambda *refs: None,
        in_specs=[anywhere] * (len(values) + len(earlier)),
        out_specs=[anywhere] * len(values),
        out_shape=[jax.ShapeDtypeStruct(v.shape, v.dtype) for v in values],
        input_output_aliases={i: i for i in range(len(values))},
        cost_estimate=pl.CostEstimate(flops=0, bytes_accessed=0, transcendentals=0),
        name="after",
    )(*values, *earlier)


def per_device(tables, features, proj_weight, gate_q, gate_k, filter_spec):
    ctx_size = lax.axis_size("ctx")
    ch_size = lax.axis_size("ch")
    plane = plane_size(ctx_size)
    lines = ctx_size // plane
    me = lax.axis_index("ctx")
    ch_me = lax.axis_index("ch")
    line_at, plane_at = me // plane, me % plane
    tok_rows, feat_cols = features.shape
    weight_rows, group_channels = proj_weight.shape
    wide = group_channels // plane
    channels = wide // lines
    freq_local = filter_spec.shape[1]
    tie = after if channels % 128 == 0 else lambda values, earlier: values

    plane_groups = [[z * plane + p for p in range(plane)] for z in range(lines)]
    onward = [(i, (i + plane) % ctx_size) for i in range(ctx_size)]

    def swap(value, d):
        perm = [(i, i // plane * plane + (i % plane ^ d)) for i in range(ctx_size)]
        return lax.ppermute(value, "ctx", perm)

    def other_core(value, e):
        return lax.ppermute(value, "ch", [(i, (i + e) % ch_size) for i in range(ch_size)])

    weight = proj_weight.reshape(weight_rows, plane, wide).transpose(1, 0, 2)
    weight = lax.all_to_all(weight, "ctx", 0, 0, tiled=True, axis_index_groups=plane_groups)
    along = [weight]

    halves = jnp.split(features, 2, axis=1)
    held = [{0: half} for half in halves]
    arrival = [[0], [0]]
    bits = [1 << b for b in range(plane.bit_length() - 1)]
    rounds = [
        (turn, k) for turn in range(len(bits)) for k in reversed(range(1 << turn))
    ]

    def feature_round(turn, k, beside):
        ds = [bits[(turn + at) % len(bits)] for at in range(2)]
        sources = [arrival[at][k] for at in range(2)]
        values = [held[at][sources[at]] for at in range(2)]
        if sources[0]:
            values = tie(values, beside)
        new = []
        for at in range(2):
            held[at][sources[at]] = values[at]
            place = sources[at] ^ ds[at]
            held[at][place] = swap(values[at], ds[at])
            new.append(held[at][place])
        if k == 0:
            arrival[:] = [sorted(held[at], key=list(held[at]).index) for at in range(2)]
        return new

    gate_blocks = gate_k.reshape(tok_rows, plane, wide)
    gates = [
        lax.dynamic_index_in_dim(gate_blocks, plane_at ^ d, 1, keepdims=False) for d in range(plane)
    ]
    spread = [spread_spectrum(filter_spec, at, plane, lines) for at in range(freq_local)]
    beside = []
    for step in range(max(lines - 1, len(rounds))):
        if step < lines - 1:
            along[-1] = tie(along[-1:], beside)[0]
            along.append(lax.ppermute(along[-1], "ctx", onward))
        if step < len(rounds):
            beside = feature_round(*rounds[step], beside + along[step : step + 1])
        beside = beside + spread[step : step + 1] + (gates if step == 1 else [])
    gates = tie(gates, along[-1:])
    gates = [swap(gate, d) if d else gate for d, gate in enumerate(gates)]

    first = tie(spread[:1], along[-1:] + beside)
    spectra = [lax.all_to_all(first[0], "ctx", 0, 0, tiled=True)]

    place = jnp.stack([line_at, plane_at, ch_me]).astype(jnp.int32)
    own = [[held[at][d] for at in range(2)] for d in range(plane)]
    pieces = [own] + [
        [[other_core(half, e) for half in d] for d in own] for e in range(1, ch_size)
    ]
    fits = channels % 128 == 0 and ch_size == 2 and feat_cols // 2 % weight_rows == 0
    if fits and weight_rows % 16 == 0 and tok_rows % 16 == 0:
        projected = project_fused(place, along, pieces, gates)
    else:
        projected = project_plain(place, along, pieces, gates)
    signals = [projected[0]] + [
        lax.ppermute(projected[k], "ctx", [(i, (i + k * plane) % ctx_size) for i in range(ctx_size)])
        for k in range(1, lines)
    ]
    for at in range(1, freq_local):
        later = tie(spread[at : at + 1], spectra[-1:] + signals[1:])
        spectra.append(lax.all_to_all(later[0], "ctx", 0, 0, tiled=True))

    if channels % 128 == 0:
        convolved = convolve_fused(place, signals, spectra, tables)
    else:
        spectrum = jnp.stack(spectra, 1).reshape(ctx_size * freq_local, 2, tok_rows, channels)
        signal = jnp.stack(signals)[jnp.mod(line_at - jnp.arange(lines), lines)]
        convolved = convolve_plain(signal.reshape(ctx_size, tok_rows, channels), spectrum)
    returned = lax.all_to_all(convolved, "ctx", 0, 0, tiled=True)
    return gate_output(returned, gate_q, plane, lines)


def solution(mesh):
    ctx_size = mesh.shape["ctx"]

    def whole(features, proj_weight, gate_q, gate_k, filter_spec):
        freq_local = filter_spec.shape[1] // ctx_size
        tables = [
            transform_tables(ctx_size, features.shape[0] // ctx_size, at, freq_local)
            for at in range(freq_local)
        ]
        return jax.shard_map(
            functools.partial(per_device, tables),
            mesh=mesh,
            in_specs=(
                P("ctx", "ch"),
                P("ctx", "ch"),
                P("ctx", "ch"),
                P("ctx", "ch"),
                P(None, "ctx", None, "ch"),
            ),
            out_specs=P("ctx", "ch"),
            check_vma=False,
        )(features, proj_weight, gate_q, gate_k, filter_spec)

    return whole
```

```python
import functools
import math

import jax
import jax.numpy as jnp
import numpy as np
from jax import lax
from jax.experimental import pallas as pl
from jax.experimental.pallas import tpu as pltpu
from jax.sharding import PartitionSpec as P

BF16 = jnp.bfloat16
F32 = jnp.float32
VMEM_LIMIT = 56 * 1024 * 1024
TIME_TILE = 16
FREQ_CHUNK = 4
PRODUCT_CHUNK = 2


def plane_size(ctx_size):
    size = 1
    while ctx_size % (2 * size) == 0 and 4 * size * size <= ctx_size:
        size *= 2
    return size


def best_scale(values):
    distinct, counts = np.unique(np.round(np.abs(values), 12), return_counts=True)
    best, best_error = 1.0, None
    for factor in np.linspace(1.0, 2.0, 2000, endpoint=False):
        scaled = distinct * factor
        rounded = scaled.astype(jnp.bfloat16).astype(np.float64)
        error = float((counts * (rounded - scaled) ** 2).sum()) / factor**2
        if best_error is None or error < best_error:
            best, best_error = float(factor), error
    return best


def split_table(table):
    high = table.astype(jnp.bfloat16)
    low = (table - high.astype(np.float64)).astype(jnp.bfloat16)
    return high, low


def transform_tables(slab_count, tok_rows, first, stride):
    freq_count = 2 * slab_count
    length = freq_count * tok_rows
    freq = np.arange(first, freq_count, stride)
    slab = np.arange(slab_count)
    fine = np.arange(TIME_TILE)
    group = np.arange(tok_rows // TIME_TILE)
    turns = (freq[:, None, None] * slab[None, None, :] % freq_count) / freq_count + (
        freq[:, None, None] * fine[None, :, None]
    ) / length
    phase = np.exp(-2j * np.pi * turns)
    slab_table = np.zeros((len(freq), 2, TIME_TILE, slab_count, TIME_TILE))
    for u in range(TIME_TILE):
        slab_table[:, 0, u, :, u] = phase[:, u].real
        slab_table[:, 1, u, :, u] = phase[:, u].imag
    slab_table = slab_table.reshape(len(freq) * 2 * TIME_TILE, slab_count * TIME_TILE)
    row = np.arange(tok_rows)
    turns = (row[:, None] * row[None, :] % tok_rows) / tok_rows
    cosine, sine = np.cos(2 * np.pi * turns), np.sin(2 * np.pi * turns)
    forward_rows = np.block([[cosine, sine], [-sine, cosine]])
    scale = best_scale(forward_rows)
    forward_rows = forward_rows * scale
    coarse = np.exp(-2j * np.pi * (freq[:, None] * TIME_TILE * group[None, :] % length) / length)
    coarse = np.stack([coarse.real, coarse.imag], axis=-1)
    inverse_scale = 1.0 / (length * scale * scale)
    return {
        "slab": split_table(slab_table),
        "slab_back": split_table(slab_table.T),
        "rows": forward_rows.astype(jnp.bfloat16),
        "rows_back": forward_rows.T.astype(jnp.bfloat16),
        "coarse": coarse.astype(np.float32).reshape(-1),
        "coarse_back": (coarse * inverse_scale).astype(np.float32).reshape(-1),
    }


def coarse_turn(ref, groups, freq, group):
    at = 2 * (freq * groups + group)
    return ref[at], ref[at + 1]


def slab_stage(coarse_ref, signal_ref, high_ref, low_ref, work_ref):
    slab_count, tok_rows, channels = signal_ref.shape
    freq_count = work_ref.shape[0]
    groups = tok_rows // TIME_TILE
    tile = TIME_TILE

    @pl.loop(0, groups // 2)
    def _(pair):
        parts = []
        for half in range(2):
            start = pl.multiple_of((2 * pair + half) * tile, tile)
            piece = signal_ref[:, pl.ds(start, tile), :]
            parts.append(piece.reshape(slab_count * tile, channels))
        block = jnp.concatenate(parts, axis=1)
        summed = jnp.dot(high_ref[...], block, preferred_element_type=F32)
        summed += jnp.dot(low_ref[...], block, preferred_element_type=F32)
        for freq in range(freq_count):
            base = freq * 2 * tile
            for half in range(2):
                lanes = slice(half * channels, (half + 1) * channels)
                real = summed[base : base + tile, lanes]
                imag = summed[base + tile : base + 2 * tile, lanes]
                cos, sin = coarse_turn(coarse_ref, groups, freq, 2 * pair + half)
                start = pl.multiple_of((2 * pair + half) * tile, tile)
                work_ref[freq, 0, pl.ds(start, tile), :] = (real * cos - imag * sin).astype(BF16)
                work_ref[freq, 1, pl.ds(start, tile), :] = (real * sin + imag * cos).astype(BF16)


def rows_stage(work_ref, rows_ref, first):
    _, _, tok_rows, channels = work_ref.shape
    wide = [work_ref[first + at].reshape(2 * tok_rows, channels) for at in range(FREQ_CHUNK)]
    return jnp.dot(rows_ref[...], jnp.concatenate(wide, axis=1), preferred_element_type=F32)


def product_and_back(forward, spectrum_refs, rows_back_ref, coarse_back_ref, work_ref, rest_ref, first):
    _, _, tok_rows, channels = work_ref.shape
    groups = tok_rows // TIME_TILE
    for chunk in range(0, FREQ_CHUNK, PRODUCT_CHUNK):
        products = []
        for at in range(chunk, chunk + PRODUCT_CHUNK):
            real, imag = forward(at)
            spec_real, spec_imag = (
                jnp.concatenate([ref[at, part].astype(F32) for ref in spectrum_refs], axis=0)
                for part in range(2)
            )
            products.append(
                jnp.concatenate(
                    [
                        (spec_real * real - spec_imag * imag).astype(BF16),
                        (spec_real * imag + spec_imag * real).astype(BF16),
                    ],
                    axis=0,
                )
            )
        inverse = jnp.dot(
            rows_back_ref[...], jnp.concatenate(products, axis=1), preferred_element_type=F32
        )
        for at in range(chunk, chunk + PRODUCT_CHUNK):
            lanes = slice((at - chunk) * channels, (at - chunk + 1) * channels)
            for group in range(groups):
                rows = slice(group * TIME_TILE, (group + 1) * TIME_TILE)
                real = inverse[rows, lanes]
                imag = inverse[tok_rows + rows.start : tok_rows + rows.stop, lanes]
                cos, sin = coarse_turn(coarse_back_ref, groups, first + at, group)
                for part, value in enumerate((real * cos + imag * sin, imag * cos - real * sin)):
                    high = value.astype(BF16)
                    work_ref[first + at, part, rows, :] = high
                    rest_ref[first + at, part, rows, :] = (value - high.astype(F32)).astype(BF16)


def slab_back_stage(work_ref, rest_ref, high_ref, low_ref, others, out_ref):
    slab_count, tok_rows, channels = out_ref.shape
    freq_count = work_ref.shape[0]
    tile = TIME_TILE
    depth = freq_count * 2 * tile

    width = max(w for w in (1, 2, 4, 8) if tok_rows // tile % w == 0)

    @pl.loop(0, tok_rows // tile // width)
    def _(turn):
        highs, lows = [], []
        for at in range(width):
            start = pl.multiple_of((width * turn + at) * tile, tile)
            highs.append(work_ref[:, :, pl.ds(start, tile), :].reshape(depth, channels))
            lows.append(rest_ref[:, :, pl.ds(start, tile), :].reshape(depth, channels))
        high = jnp.concatenate(highs, axis=1)
        low = jnp.concatenate(lows, axis=1)
        total = jnp.dot(high_ref[...], high, preferred_element_type=F32)
        total += jnp.dot(low_ref[...], high, preferred_element_type=F32)
        total += jnp.dot(high_ref[...], low, preferred_element_type=F32)
        for at in range(width):
            start = pl.multiple_of((width * turn + at) * tile, tile)
            lanes = slice(at * channels, (at + 1) * channels)
            value = total[:, lanes].reshape(slab_count, tile, channels)
            for other in others:
                value += other[:, pl.ds(start, tile), :]
            out_ref[:, pl.ds(start, tile), :] = value.astype(out_ref.dtype)


def gather_signal(place_ref, piece_refs, signal_ref):
    lines = len(piece_refs)
    for k, ref in enumerate(piece_refs):
        line = lax.rem(place_ref[0] + lines - k, lines)
        signal_ref[pl.ds(line * ref.shape[0], ref.shape[0])] = ref[...]


def convolve_kernel(lines, place_ref, coarse_ref, coarse_back_ref, *refs):
    piece_refs, refs = refs[:lines], refs[lines:]
    spectrum_ref, slab_high_ref, slab_low_ref, back_high_ref, back_low_ref = refs[:5]
    rows_ref, rows_back_ref, out_ref, signal_ref, work_ref, rest_ref = refs[5:]
    _, tok_rows, channels = signal_ref.shape
    step = pl.program_id(0)

    @pl.when(step == 0)
    def _():
        gather_signal(place_ref, piece_refs, signal_ref)
        slab_stage(coarse_ref, signal_ref, slab_high_ref, slab_low_ref, work_ref)

    first = step * FREQ_CHUNK
    transformed = rows_stage(work_ref, rows_ref, first)

    def forward(at):
        lanes = slice(at * channels, (at + 1) * channels)
        return transformed[:tok_rows, lanes], transformed[tok_rows:, lanes]

    product_and_back(forward, [spectrum_ref], rows_back_ref, coarse_back_ref, work_ref, rest_ref, first)

    @pl.when(step == pl.num_programs(0) - 1)
    def _():
        slab_back_stage(work_ref, rest_ref, back_high_ref, back_low_ref, [], out_ref)


def forward_kernel(lines, place_ref, coarse_ref, *refs):
    piece_refs, refs = refs[:lines], refs[lines:]
    slab_high_ref, slab_low_ref, rows_ref, out_ref, signal_ref, work_ref = refs
    _, tok_rows, channels = signal_ref.shape
    step = pl.program_id(0)

    @pl.when(step == 0)
    def _():
        gather_signal(place_ref, piece_refs, signal_ref)
        slab_stage(coarse_ref, signal_ref, slab_high_ref, slab_low_ref, work_ref)

    transformed = rows_stage(work_ref, rows_ref, step * FREQ_CHUNK)
    for at in range(FREQ_CHUNK):
        lanes = slice(at * channels, (at + 1) * channels)
        out_ref[at, 0] = transformed[:tok_rows, lanes]
        out_ref[at, 1] = transformed[tok_rows:, lanes]


def inverse_kernel(coarse_back_ref, forward_ref, *refs):
    *spectrum_refs, back_high_ref, back_low_ref, rows_back_ref, other_ref = refs[:-3]
    out_ref, work_ref, rest_ref = refs[-3:]
    step = pl.program_id(0)

    def forward(at):
        return forward_ref[at, 0], forward_ref[at, 1]

    product_and_back(
        forward, spectrum_refs, rows_back_ref, coarse_back_ref, work_ref, rest_ref, step * FREQ_CHUNK
    )

    @pl.when(step == pl.num_programs(0) - 1)
    def _():
        slab_back_stage(work_ref, rest_ref, back_high_ref, back_low_ref, [other_ref], out_ref)


def whole_block(array):
    return pl.BlockSpec(array.shape, lambda i: (0,) * array.ndim)


def frequency_call(kernel, name, freq_count, operands, out_shape, out_blocked, scratch, flops):
    arrays, specs = [], []

    def blocked(shape):
        return pl.BlockSpec((FREQ_CHUNK,) + shape[1:], lambda i: (i,) + (0,) * (len(shape) - 1))

    for array, kind in operands:
        array = jnp.asarray(array)
        arrays.append(array)
        if kind == "scalar":
            specs.append(pl.BlockSpec(memory_space=pltpu.SMEM))
        else:
            specs.append(blocked(array.shape) if kind == "blocked" else whole_block(array))
    moved = sum(a.size * a.dtype.itemsize for a in arrays)
    return pl.pallas_call(
        kernel,
        grid=(freq_count // FREQ_CHUNK,),
        in_specs=specs,
        out_specs=blocked(out_shape.shape) if out_blocked else whole_block(out_shape),
        out_shape=out_shape,
        scratch_shapes=scratch,
        compiler_params=pltpu.CompilerParams(
            dimension_semantics=("arbitrary",), vmem_limit_bytes=VMEM_LIMIT
        ),
        cost_estimate=pl.CostEstimate(flops=flops, bytes_accessed=moved, transcendentals=0),
        name=name,
    )(*arrays)


def convolve_fused(place, pieces, spectra, tables):
    lines = len(pieces)
    plane, tok_rows, channels = pieces[0].shape
    slab_count = lines * plane
    signal = jax.ShapeDtypeStruct((slab_count, tok_rows, channels), BF16)
    gathered = pltpu.VMEM(signal.shape, BF16)
    freq_count = spectra[0].shape[0]
    rows_flops = 2 * freq_count * channels * (2 * tok_rows) ** 2
    slab_flops = 4 * freq_count * channels * tok_rows * slab_count * TIME_TILE
    work = pltpu.VMEM((freq_count, 2, tok_rows, channels), BF16)
    total = None
    for spectrum, table in zip(spectra[:-1], tables[:-1]):
        part = frequency_call(
            functools.partial(convolve_kernel, lines),
            "convolve",
            freq_count,
            [
                (place, "scalar"),
                (table["coarse"], "scalar"),
                (table["coarse_back"], "scalar"),
                *[(piece, "whole") for piece in pieces],
                (spectrum, "blocked"),
                *[(t, "whole") for t in table["slab"]],
                *[(t, "whole") for t in table["slab_back"]],
                (table["rows"], "whole"),
                (table["rows_back"], "whole"),
            ],
            jax.ShapeDtypeStruct(signal.shape, F32),
            False,
            [gathered, work, work],
            2 * rows_flops + 5 * slab_flops,
        )
        total = part if total is None else total + part
    if total is None:
        total = jnp.zeros(signal.shape, F32)
    table = tables[-1]
    forward = frequency_call(
        functools.partial(forward_kernel, lines),
        "forward",
        freq_count,
        [
            (place, "scalar"),
            (table["coarse"], "scalar"),
            *[(piece, "whole") for piece in pieces],
            *[(t, "whole") for t in table["slab"]],
            (table["rows"], "whole"),
        ],
        jax.ShapeDtypeStruct((freq_count, 2, tok_rows, channels), F32),
        True,
        [gathered, work],
        rows_flops + 2 * slab_flops,
    )
    return frequency_call(
        inverse_kernel,
        "inverse",
        freq_count,
        [
            (table["coarse_back"], "scalar"),
            (forward, "blocked"),
            *[(part, "blocked") for part in spectra[-1]],
            *[(t, "whole") for t in table["slab_back"]],
            (table["rows_back"], "whole"),
            (total, "whole"),
        ],
        jax.ShapeDtypeStruct(signal.shape, BF16),
        False,
        [work, work],
        rows_flops + 3 * slab_flops,
    )


def spread_kernel(plane, lines, channels, values_ref, out_ref):
    for at in range(plane):
        for line in range(lines):
            first = (at * lines + line) * channels
            out_ref[line, at, 0] = values_ref[0, 0, :, first : first + channels].astype(BF16)


def spread_spectrum(filter_spec, at, first, rows, plane, lines):
    parts, _, _, group_channels = filter_spec.shape
    channels = group_channels // (plane * lines)
    if channels % 128:
        spec = filter_spec[:, at, first : first + rows].reshape(parts, rows, plane, lines, channels)
        return spec.transpose(3, 2, 0, 1, 4).astype(BF16)
    block = max(r for r in range(16, 97, 16) if rows % r == 0 and first % r == 0)
    return pl.pallas_call(
        functools.partial(spread_kernel, plane, lines, channels),
        grid=(parts, rows // block),
        in_specs=[
            pl.BlockSpec((1, 1, block, group_channels), lambda i, j: (i, at, first // block + j, 0))
        ],
        out_specs=pl.BlockSpec((lines, plane, 1, block, channels), lambda i, j: (0, 0, i, j, 0)),
        out_shape=jax.ShapeDtypeStruct((lines, plane, parts, rows, channels), BF16),
        compiler_params=pltpu.CompilerParams(
            dimension_semantics=("arbitrary", "arbitrary"), vmem_limit_bytes=VMEM_LIMIT
        ),
        cost_estimate=pl.CostEstimate(
            flops=0, bytes_accessed=6 * parts * rows * group_channels, transcendentals=0
        ),
        name="spread_spectrum",
    )(filter_spec)


def gate_kernel(lines, channels, values_ref, gate_ref, out_ref):
    for line in range(lines):
        lanes = slice(line * channels, (line + 1) * channels)
        value = gate_ref[:, lanes].astype(F32) * values_ref[line, 0].astype(F32)
        out_ref[:, lanes] = value.astype(BF16)


def gate_output(returned, gate_q, plane, lines):
    _, tok_rows, channels = returned.shape
    returned = returned.reshape(lines, plane, tok_rows, channels)
    if channels % 128:
        returned = returned.transpose(2, 1, 0, 3).reshape(gate_q.shape)
        return (gate_q.astype(F32) * returned.astype(F32)).astype(BF16)
    flat = pl.BlockSpec((tok_rows, lines * channels), lambda i: (0, i))
    return pl.pallas_call(
        functools.partial(gate_kernel, lines, channels),
        grid=(plane,),
        in_specs=[pl.BlockSpec((lines, 1, tok_rows, channels), lambda i: (0, i, 0, 0)), flat],
        out_specs=flat,
        out_shape=jax.ShapeDtypeStruct(gate_q.shape, BF16),
        compiler_params=pltpu.CompilerParams(
            dimension_semantics=("arbitrary",), vmem_limit_bytes=VMEM_LIMIT
        ),
        cost_estimate=pl.CostEstimate(
            flops=gate_q.size, bytes_accessed=6 * gate_q.size, transcendentals=0
        ),
        name="gate_output",
    )(returned, gate_q)


def convolve_plain(signal, spectrum):
    slab_count, tok_rows, channels = signal.shape
    freq_count = 2 * slab_count
    length = freq_count * tok_rows

    def phase(left, right, modulus):
        turns = (left[:, None] * right[None, :] % modulus).astype(F32) * (2.0 * math.pi / modulus)
        return jnp.cos(turns), jnp.sin(turns)

    dot = functools.partial(jnp.einsum, precision=lax.Precision.HIGH, preferred_element_type=F32)
    freq = jnp.arange(freq_count, dtype=jnp.int32)
    slab = jnp.arange(slab_count, dtype=jnp.int32)
    row = jnp.arange(tok_rows, dtype=jnp.int32)
    slab_cos, slab_sin = phase(freq, slab, freq_count)
    turn_cos, turn_sin = (part[:, :, None] for part in phase(freq, row, length))
    row_cos, row_sin = phase(row, row, tok_rows)
    values = signal.astype(F32)
    real, imag = dot("ks,stc->ktc", slab_cos, values), -dot("ks,stc->ktc", slab_sin, values)
    real, imag = real * turn_cos + imag * turn_sin, imag * turn_cos - real * turn_sin
    real, imag = (
        dot("jt,ktc->kjc", row_cos, real) + dot("jt,ktc->kjc", row_sin, imag),
        dot("jt,ktc->kjc", row_cos, imag) - dot("jt,ktc->kjc", row_sin, real),
    )
    spec_real, spec_imag = spectrum[:, 0].astype(F32), spectrum[:, 1].astype(F32)
    real, imag = real * spec_real - imag * spec_imag, imag * spec_real + real * spec_imag
    real, imag = (
        dot("jt,ktc->kjc", row_cos, real) - dot("jt,ktc->kjc", row_sin, imag),
        dot("jt,ktc->kjc", row_cos, imag) + dot("jt,ktc->kjc", row_sin, real),
    )
    real, imag = real * turn_cos - imag * turn_sin, imag * turn_cos + real * turn_sin
    values = dot("ks,ktc->stc", slab_cos, real) - dot("ks,ktc->stc", slab_sin, imag)
    return (values / length).astype(BF16)


def project_kernel(lines, plane, place_ref, *refs):
    along_refs, refs = refs[:lines], refs[lines:]
    feature_refs, refs = refs[: 4 * plane], refs[4 * plane :]
    gate_refs, (out_ref, weight_ref) = refs[:plane], refs[plane:]
    line_at, plane_at, core = place_ref[0], place_ref[1], place_ref[2]
    for k in range(lines):
        line = lax.rem(line_at + lines - k, lines)
        weight_ref[pl.ds(line * plane, plane)] = along_refs[k][...]
    _, weight_rows, wide = weight_ref.shape
    depth = feature_refs[0].shape[1]
    channels = out_ref.shape[3]
    blocks = depth // weight_rows
    for d in range(plane):
        total = None
        for e in range(2):
            for half in range(2):
                first = (2 * lax.rem(core + e, 2) + half) * blocks
                weights = weight_ref[pl.ds(first, blocks)].reshape(depth, wide)
                features = feature_refs[(e * plane + d) * 2 + half][...]
                term = jnp.dot(features, weights, preferred_element_type=F32)
                total = term if total is None else total + term
        value = (gate_refs[d][...].astype(F32) * total).astype(BF16)
        for line in range(lines):
            onward = lax.rem(line + lines - line_at, lines)
            out_ref[onward, plane_at ^ d] = value[:, line * channels : (line + 1) * channels]


def project_fused(place, along, pieces, gates):
    lines, plane = len(along), len(gates)
    _, weight_rows, wide = along[0].shape
    tok_rows = gates[0].shape[0]
    flat = [half for core in pieces for d in core for half in d]
    operands = [*along, *flat, *gates]
    local = pl.BlockSpec(memory_space=pltpu.VMEM)
    return pl.pallas_call(
        functools.partial(project_kernel, lines, plane),
        in_specs=[pl.BlockSpec(memory_space=pltpu.SMEM)] + [local] * len(operands),
        out_specs=local,
        out_shape=jax.ShapeDtypeStruct((lines, plane, tok_rows, wide // lines), BF16),
        scratch_shapes=[pltpu.VMEM((lines * plane, weight_rows, wide), BF16)],
        compiler_params=pltpu.CompilerParams(vmem_limit_bytes=VMEM_LIMIT),
        cost_estimate=pl.CostEstimate(
            flops=2 * wide * sum(f.size for f in flat),
            bytes_accessed=2 * sum(o.size for o in operands),
            transcendentals=0,
        ),
        name="project",
    )(place, *operands)


def project_plain(place, along, pieces, gates):
    line_at, plane_at, core = place[0], place[1], place[2]
    lines = len(along)
    pieces = [jnp.stack([jnp.stack(d) for d in by_core]) for by_core in pieces]
    gates = jnp.stack(gates)
    plane, _, tok_rows, depth = pieces[0].shape
    wide = along[0].shape[2]
    take_line = jnp.mod(line_at - jnp.arange(lines), lines)
    take_plane = jnp.arange(plane) ^ plane_at
    weight = jnp.stack(along)[take_line].reshape(len(pieces), 2, depth, wide)
    total = jnp.zeros((plane, tok_rows, wide), F32)
    for e, piece in enumerate(pieces):
        at = jnp.mod(core - e, len(pieces))
        total += jnp.einsum("phtk,hkc->ptc", piece, weight[at], preferred_element_type=F32)
    value = (gates.astype(F32) * total).astype(BF16)[take_plane]
    value = value.reshape(plane, tok_rows, lines, wide // lines).transpose(2, 0, 1, 3)
    return value[jnp.mod(line_at + jnp.arange(lines), lines)]


def after(values, earlier):
    values, earlier = list(values), list(earlier)
    if not earlier:
        return values
    anywhere = pl.BlockSpec(memory_space=pl.ANY)
    return pl.pallas_call(
        lambda *refs: None,
        in_specs=[anywhere] * (len(values) + len(earlier)),
        out_specs=[anywhere] * len(values),
        out_shape=[jax.ShapeDtypeStruct(v.shape, v.dtype) for v in values],
        input_output_aliases={i: i for i in range(len(values))},
        cost_estimate=pl.CostEstimate(flops=0, bytes_accessed=0, transcendentals=0),
        name="after",
    )(*values, *earlier)


def per_device(tables, features, proj_weight, gate_q, gate_k, filter_spec):
    ctx_size = lax.axis_size("ctx")
    ch_size = lax.axis_size("ch")
    plane = plane_size(ctx_size)
    lines = ctx_size // plane
    me = lax.axis_index("ctx")
    ch_me = lax.axis_index("ch")
    line_at, plane_at = me // plane, me % plane
    tok_rows, feat_cols = features.shape
    weight_rows, group_channels = proj_weight.shape
    wide = group_channels // plane
    channels = wide // lines
    freq_local = filter_spec.shape[1]
    tie = after if channels % 128 == 0 else lambda values, earlier: values

    plane_groups = [[z * plane + p for p in range(plane)] for z in range(lines)]
    onward = [(i, (i + plane) % ctx_size) for i in range(ctx_size)]

    def swap(value, d):
        perm = [(i, i // plane * plane + (i % plane ^ d)) for i in range(ctx_size)]
        return lax.ppermute(value, "ctx", perm)

    def other_core(value, e):
        return lax.ppermute(value, "ch", [(i, (i + e) % ch_size) for i in range(ch_size)])

    def line_shift(value, k):
        return lax.ppermute(value, "ctx", [(i, (i + k * plane) % ctx_size) for i in range(ctx_size)])

    early_rows = tok_rows // 4 // 16 * 16
    early = spread_spectrum(filter_spec, freq_local - 1, 0, early_rows, plane, lines)
    early = [
        lax.dynamic_index_in_dim(early, jnp.mod(line_at + k, lines), 0, keepdims=False)
        for k in range(lines)
    ]
    early = [line_shift(piece, k) if k else piece for k, piece in enumerate(early)]

    weight = proj_weight.reshape(weight_rows, plane, wide).transpose(1, 0, 2)
    weight = lax.all_to_all(weight, "ctx", 0, 0, tiled=True, axis_index_groups=plane_groups)
    along = list(tie([weight], early[1:]))

    halves = jnp.split(features, 2, axis=1)
    held = [{0: half} for half in halves]
    arrival = [[0], [0]]
    bits = [1 << b for b in range(plane.bit_length() - 1)]
    rounds = [
        (turn, k) for turn in range(len(bits)) for k in reversed(range(1 << turn))
    ]

    def feature_round(turn, k, beside):
        ds = [bits[(turn + at) % len(bits)] for at in range(2)]
        sources = [arrival[at][k] for at in range(2)]
        values = [held[at][sources[at]] for at in range(2)]
        if sources[0]:
            values = tie(values, beside)
        new = []
        for at in range(2):
            held[at][sources[at]] = values[at]
            place = sources[at] ^ ds[at]
            held[at][place] = swap(values[at], ds[at])
            new.append(held[at][place])
        if k == 0:
            arrival[:] = [sorted(held[at], key=list(held[at]).index) for at in range(2)]
        return new

    gate_blocks = gate_k.reshape(tok_rows, plane, wide)
    gates = [
        lax.dynamic_index_in_dim(gate_blocks, plane_at ^ d, 1, keepdims=False) for d in range(plane)
    ]
    skipped = [0] * (freq_local - 1) + [early_rows]
    spread = [
        spread_spectrum(filter_spec, at, skip, tok_rows - skip, plane, lines)
        for at, skip in enumerate(skipped)
    ]
    spread = [spec.reshape((ctx_size,) + spec.shape[2:]) for spec in spread]
    beside = []
    for step in range(max(lines - 1, len(rounds))):
        if step < lines - 1:
            along[-1] = tie(along[-1:], beside)[0]
            along.append(lax.ppermute(along[-1], "ctx", onward))
        if step < len(rounds):
            beside = feature_round(*rounds[step], beside + along[step : step + 1])
        beside = beside + spread[step : step + 1] + (gates if step == 1 else [])
    gates = tie(gates, along[-1:])
    gates = [swap(gate, d) if d else gate for d, gate in enumerate(gates)]

    first = tie(spread[:1], along[-1:] + beside)
    spectra = [lax.all_to_all(first[0], "ctx", 0, 0, tiled=True)]

    place = jnp.stack([line_at, plane_at, ch_me]).astype(jnp.int32)
    own = [[held[at][d] for at in range(2)] for d in range(plane)]
    pieces = [own] + [
        [[other_core(half, e) for half in d] for d in own] for e in range(1, ch_size)
    ]
    fits = channels % 128 == 0 and ch_size == 2 and feat_cols // 2 % weight_rows == 0
    if fits and weight_rows % 16 == 0 and tok_rows % 16 == 0:
        projected = project_fused(place, along, pieces, gates)
    else:
        projected = project_plain(place, along, pieces, gates)
    signals = [projected[0]] + [line_shift(projected[k], k) for k in range(1, lines)]

    early = [
        jnp.stack([lax.dynamic_index_in_dim(piece, plane_at ^ d, 0, keepdims=False) for piece in early])
        for d in range(plane)
    ]
    early = tie(early, signals[1:])
    early = jnp.stack([swap(piece, d) if d else piece for d, piece in enumerate(early)])
    from_plane = (jnp.arange(plane) ^ plane_at)[None, :]
    early = early[from_plane, jnp.mod(line_at - jnp.arange(lines), lines)[:, None]]
    early = early.reshape((ctx_size,) + early.shape[2:])
    for at in range(1, freq_local):
        later = tie(spread[at : at + 1], spectra[-1:] + signals[1:])
        spectra.append(lax.all_to_all(later[0], "ctx", 0, 0, tiled=True))

    spectra[-1] = [early, spectra[-1]]
    if channels % 128 == 0:
        convolved = convolve_fused(place, signals, spectra, tables)
    else:
        spectra[-1] = jnp.concatenate(spectra[-1], axis=2)
        spectrum = jnp.stack(spectra, 1).reshape(ctx_size * freq_local, 2, tok_rows, channels)
        signal = jnp.stack(signals)[jnp.mod(line_at - jnp.arange(lines), lines)]
        convolved = convolve_plain(signal.reshape(ctx_size, tok_rows, channels), spectrum)
    returned = lax.all_to_all(convolved, "ctx", 0, 0, tiled=True)
    return gate_output(returned, gate_q, plane, lines)


def solution(mesh):
    ctx_size = mesh.shape["ctx"]

    def whole(features, proj_weight, gate_q, gate_k, filter_spec):
        freq_local = filter_spec.shape[1] // ctx_size
        tables = [
            transform_tables(ctx_size, features.shape[0] // ctx_size, at, freq_local)
            for at in range(freq_local)
        ]
        return jax.shard_map(
            functools.partial(per_device, tables),
            mesh=mesh,
            in_specs=(
                P("ctx", "ch"),
                P("ctx", "ch"),
                P("ctx", "ch"),
                P("ctx", "ch"),
                P(None, "ctx", None, "ch"),
            ),
            out_specs=P("ctx", "ch"),
            check_vma=False,
        )(features, proj_weight, gate_q, gate_k, filter_spec)

    return whole
```

```python
import functools
import math

import jax
import jax.numpy as jnp
import numpy as np
from jax import lax
from jax.experimental import pallas as pl
from jax.experimental.pallas import tpu as pltpu
from jax.sharding import PartitionSpec as P

BF16 = jnp.bfloat16
F32 = jnp.float32
VMEM_LIMIT = 56 * 1024 * 1024
TIME_TILE = 16
FREQ_CHUNK = 4
PRODUCT_CHUNK = 2


def plane_size(ctx_size):
    size = 1
    while ctx_size % (2 * size) == 0 and 4 * size * size <= ctx_size:
        size *= 2
    return size


def best_scale(values):
    distinct, counts = np.unique(np.round(np.abs(values), 12), return_counts=True)
    best, best_error = 1.0, None
    for factor in np.linspace(1.0, 2.0, 2000, endpoint=False):
        scaled = distinct * factor
        rounded = scaled.astype(jnp.bfloat16).astype(np.float64)
        error = float((counts * (rounded - scaled) ** 2).sum()) / factor**2
        if best_error is None or error < best_error:
            best, best_error = float(factor), error
    return best


def split_table(table):
    high = table.astype(jnp.bfloat16)
    low = (table - high.astype(np.float64)).astype(jnp.bfloat16)
    return high, low


def transform_tables(slab_count, tok_rows, first, stride):
    freq_count = 2 * slab_count
    length = freq_count * tok_rows
    freq = np.arange(first, freq_count, stride)
    slab = np.arange(slab_count)
    fine = np.arange(TIME_TILE)
    group = np.arange(tok_rows // TIME_TILE)
    turns = (freq[:, None, None] * slab[None, None, :] % freq_count) / freq_count + (
        freq[:, None, None] * fine[None, :, None]
    ) / length
    phase = np.exp(-2j * np.pi * turns)
    slab_table = np.zeros((len(freq), 2, TIME_TILE, slab_count, TIME_TILE))
    for u in range(TIME_TILE):
        slab_table[:, 0, u, :, u] = phase[:, u].real
        slab_table[:, 1, u, :, u] = phase[:, u].imag
    slab_table = slab_table.reshape(len(freq) * 2 * TIME_TILE, slab_count * TIME_TILE)
    row = np.arange(tok_rows)
    turns = (row[:, None] * row[None, :] % tok_rows) / tok_rows
    cosine, sine = np.cos(2 * np.pi * turns), np.sin(2 * np.pi * turns)
    forward_rows = np.block([[cosine, sine], [-sine, cosine]])
    scale = best_scale(forward_rows)
    forward_rows = forward_rows * scale
    coarse = np.exp(-2j * np.pi * (freq[:, None] * TIME_TILE * group[None, :] % length) / length)
    coarse = np.stack([coarse.real, coarse.imag], axis=-1)
    inverse_scale = 1.0 / (length * scale * scale)
    return {
        "slab": split_table(slab_table),
        "slab_back": split_table(slab_table.T),
        "rows": forward_rows.astype(jnp.bfloat16),
        "rows_back": forward_rows.T.astype(jnp.bfloat16),
        "coarse": coarse.astype(np.float32).reshape(-1),
        "coarse_back": (coarse * inverse_scale).astype(np.float32).reshape(-1),
    }


def coarse_turn(ref, groups, freq, group):
    at = 2 * (freq * groups + group)
    return ref[at], ref[at + 1]


def slab_stage(coarse_ref, signal_ref, high_ref, low_ref, work_ref):
    slab_count, tok_rows, channels = signal_ref.shape
    freq_count = work_ref.shape[0]
    groups = tok_rows // TIME_TILE
    tile = TIME_TILE

    @pl.loop(0, groups // 2)
    def _(pair):
        parts = []
        for half in range(2):
            start = pl.multiple_of((2 * pair + half) * tile, tile)
            piece = signal_ref[:, pl.ds(start, tile), :]
            parts.append(piece.reshape(slab_count * tile, channels))
        block = jnp.concatenate(parts, axis=1)
        summed = jnp.dot(high_ref[...], block, preferred_element_type=F32)
        summed += jnp.dot(low_ref[...], block, preferred_element_type=F32)
        for freq in range(freq_count):
            base = freq * 2 * tile
            for half in range(2):
                lanes = slice(half * channels, (half + 1) * channels)
                real = summed[base : base + tile, lanes]
                imag = summed[base + tile : base + 2 * tile, lanes]
                cos, sin = coarse_turn(coarse_ref, groups, freq, 2 * pair + half)
                start = pl.multiple_of((2 * pair + half) * tile, tile)
                work_ref[freq, 0, pl.ds(start, tile), :] = (real * cos - imag * sin).astype(BF16)
                work_ref[freq, 1, pl.ds(start, tile), :] = (real * sin + imag * cos).astype(BF16)


def rows_stage(work_ref, rows_ref, first):
    _, _, tok_rows, channels = work_ref.shape
    wide = [work_ref[first + at].reshape(2 * tok_rows, channels) for at in range(FREQ_CHUNK)]
    return jnp.dot(rows_ref[...], jnp.concatenate(wide, axis=1), preferred_element_type=F32)


def product_and_back(forward, spectrum_refs, rows_back_ref, coarse_back_ref, work_ref, rest_ref, first):
    _, _, tok_rows, channels = work_ref.shape
    groups = tok_rows // TIME_TILE
    for chunk in range(0, FREQ_CHUNK, PRODUCT_CHUNK):
        products = []
        for at in range(chunk, chunk + PRODUCT_CHUNK):
            real, imag = forward(at)
            spec_real, spec_imag = (
                jnp.concatenate([ref[at, part].astype(F32) for ref in spectrum_refs], axis=0)
                for part in range(2)
            )
            products.append(
                jnp.concatenate(
                    [
                        (spec_real * real - spec_imag * imag).astype(BF16),
                        (spec_real * imag + spec_imag * real).astype(BF16),
                    ],
                    axis=0,
                )
            )
        inverse = jnp.dot(
            rows_back_ref[...], jnp.concatenate(products, axis=1), preferred_element_type=F32
        )
        for at in range(chunk, chunk + PRODUCT_CHUNK):
            lanes = slice((at - chunk) * channels, (at - chunk + 1) * channels)
            for group in range(groups):
                rows = slice(group * TIME_TILE, (group + 1) * TIME_TILE)
                real = inverse[rows, lanes]
                imag = inverse[tok_rows + rows.start : tok_rows + rows.stop, lanes]
                cos, sin = coarse_turn(coarse_back_ref, groups, first + at, group)
                for part, value in enumerate((real * cos + imag * sin, imag * cos - real * sin)):
                    high = value.astype(BF16)
                    work_ref[first + at, part, rows, :] = high
                    rest_ref[first + at, part, rows, :] = (value - high.astype(F32)).astype(BF16)


def slab_back_stage(work_ref, rest_ref, high_ref, low_ref, others, out_ref):
    slab_count, tok_rows, channels = out_ref.shape
    freq_count = work_ref.shape[0]
    tile = TIME_TILE
    depth = freq_count * 2 * tile

    width = max(w for w in (1, 2, 4, 8) if tok_rows // tile % w == 0)

    @pl.loop(0, tok_rows // tile // width)
    def _(turn):
        highs, lows = [], []
        for at in range(width):
            start = pl.multiple_of((width * turn + at) * tile, tile)
            highs.append(work_ref[:, :, pl.ds(start, tile), :].reshape(depth, channels))
            lows.append(rest_ref[:, :, pl.ds(start, tile), :].reshape(depth, channels))
        high = jnp.concatenate(highs, axis=1)
        low = jnp.concatenate(lows, axis=1)
        total = jnp.dot(high_ref[...], high, preferred_element_type=F32)
        total += jnp.dot(low_ref[...], high, preferred_element_type=F32)
        total += jnp.dot(high_ref[...], low, preferred_element_type=F32)
        for at in range(width):
            start = pl.multiple_of((width * turn + at) * tile, tile)
            lanes = slice(at * channels, (at + 1) * channels)
            value = total[:, lanes].reshape(slab_count, tile, channels)
            for other in others:
                value += other[:, pl.ds(start, tile), :]
            out_ref[:, pl.ds(start, tile), :] = value.astype(out_ref.dtype)


def gather_signal(place_ref, piece_refs, signal_ref):
    lines = len(piece_refs)
    for k, ref in enumerate(piece_refs):
        line = lax.rem(place_ref[0] + lines - k, lines)
        signal_ref[pl.ds(line * ref.shape[0], ref.shape[0])] = ref[...]


def convolve_kernel(lines, place_ref, coarse_ref, coarse_back_ref, *refs):
    piece_refs, refs = refs[:lines], refs[lines:]
    spectrum_ref, slab_high_ref, slab_low_ref, back_high_ref, back_low_ref = refs[:5]
    rows_ref, rows_back_ref, out_ref, signal_ref, work_ref, rest_ref = refs[5:]
    _, tok_rows, channels = signal_ref.shape
    step = pl.program_id(0)

    @pl.when(step == 0)
    def _():
        gather_signal(place_ref, piece_refs, signal_ref)
        slab_stage(coarse_ref, signal_ref, slab_high_ref, slab_low_ref, work_ref)

    first = step * FREQ_CHUNK
    transformed = rows_stage(work_ref, rows_ref, first)

    def forward(at):
        lanes = slice(at * channels, (at + 1) * channels)
        return transformed[:tok_rows, lanes], transformed[tok_rows:, lanes]

    product_and_back(forward, [spectrum_ref], rows_back_ref, coarse_back_ref, work_ref, rest_ref, first)

    @pl.when(step == pl.num_programs(0) - 1)
    def _():
        slab_back_stage(work_ref, rest_ref, back_high_ref, back_low_ref, [], out_ref)


def forward_kernel(lines, place_ref, coarse_ref, *refs):
    piece_refs, refs = refs[:lines], refs[lines:]
    slab_high_ref, slab_low_ref, rows_ref, out_ref, signal_ref, work_ref = refs
    _, tok_rows, channels = signal_ref.shape
    step = pl.program_id(0)

    @pl.when(step == 0)
    def _():
        gather_signal(place_ref, piece_refs, signal_ref)
        slab_stage(coarse_ref, signal_ref, slab_high_ref, slab_low_ref, work_ref)

    transformed = rows_stage(work_ref, rows_ref, step * FREQ_CHUNK)
    for at in range(FREQ_CHUNK):
        lanes = slice(at * channels, (at + 1) * channels)
        out_ref[at, 0] = transformed[:tok_rows, lanes]
        out_ref[at, 1] = transformed[tok_rows:, lanes]


def inverse_kernel(coarse_back_ref, forward_ref, *refs):
    *spectrum_refs, back_high_ref, back_low_ref, rows_back_ref, other_ref = refs[:-3]
    out_ref, work_ref, rest_ref = refs[-3:]
    step = pl.program_id(0)

    def forward(at):
        return forward_ref[at, 0], forward_ref[at, 1]

    product_and_back(
        forward, spectrum_refs, rows_back_ref, coarse_back_ref, work_ref, rest_ref, step * FREQ_CHUNK
    )

    @pl.when(step == pl.num_programs(0) - 1)
    def _():
        slab_back_stage(work_ref, rest_ref, back_high_ref, back_low_ref, [other_ref], out_ref)


def whole_block(array):
    return pl.BlockSpec(array.shape, lambda i: (0,) * array.ndim)


def frequency_call(kernel, name, freq_count, operands, out_shape, out_blocked, scratch, flops):
    arrays, specs = [], []

    def blocked(shape):
        return pl.BlockSpec((FREQ_CHUNK,) + shape[1:], lambda i: (i,) + (0,) * (len(shape) - 1))

    for array, kind in operands:
        array = jnp.asarray(array)
        arrays.append(array)
        if kind == "scalar":
            specs.append(pl.BlockSpec(memory_space=pltpu.SMEM))
        else:
            specs.append(blocked(array.shape) if kind == "blocked" else whole_block(array))
    moved = sum(a.size * a.dtype.itemsize for a in arrays)
    return pl.pallas_call(
        kernel,
        grid=(freq_count // FREQ_CHUNK,),
        in_specs=specs,
        out_specs=blocked(out_shape.shape) if out_blocked else whole_block(out_shape),
        out_shape=out_shape,
        scratch_shapes=scratch,
        compiler_params=pltpu.CompilerParams(
            dimension_semantics=("arbitrary",), vmem_limit_bytes=VMEM_LIMIT
        ),
        cost_estimate=pl.CostEstimate(flops=flops, bytes_accessed=moved, transcendentals=0),
        name=name,
    )(*arrays)


def convolve_fused(place, pieces, spectra, tables, early_rows):
    lines = len(pieces)
    plane, tok_rows, channels = pieces[0].shape
    slab_count = lines * plane
    signal = jax.ShapeDtypeStruct((slab_count, tok_rows, channels), BF16)
    gathered = pltpu.VMEM(signal.shape, BF16)
    freq_count = spectra[0].shape[0]
    rows_flops = 2 * freq_count * channels * (2 * tok_rows) ** 2
    slab_flops = 4 * freq_count * channels * tok_rows * slab_count * TIME_TILE
    work = pltpu.VMEM((freq_count, 2, tok_rows, channels), BF16)
    total = None
    for spectrum, table in zip(spectra[:-1], tables[:-1]):
        part = frequency_call(
            functools.partial(convolve_kernel, lines),
            "convolve",
            freq_count,
            [
                (place, "scalar"),
                (table["coarse"], "scalar"),
                (table["coarse_back"], "scalar"),
                *[(piece, "whole") for piece in pieces],
                (spectrum, "blocked"),
                *[(t, "whole") for t in table["slab"]],
                *[(t, "whole") for t in table["slab_back"]],
                (table["rows"], "whole"),
                (table["rows_back"], "whole"),
            ],
            jax.ShapeDtypeStruct(signal.shape, F32),
            False,
            [gathered, work, work],
            2 * rows_flops + 5 * slab_flops,
        )
        total = part if total is None else total + part
    if total is None:
        total = jnp.zeros(signal.shape, F32)
    table = tables[-1]
    forward = frequency_call(
        functools.partial(forward_kernel, lines),
        "forward",
        freq_count,
        [
            (place, "scalar"),
            (table["coarse"], "scalar"),
            *[(piece, "whole") for piece in pieces],
            *[(t, "whole") for t in table["slab"]],
            (table["rows"], "whole"),
        ],
        jax.ShapeDtypeStruct((freq_count, 2, tok_rows, channels), F32),
        True,
        [gathered, work],
        rows_flops + 2 * slab_flops,
    )
    return frequency_call(
        inverse_kernel,
        "inverse",
        freq_count,
        [
            (table["coarse_back"], "scalar"),
            (forward, "blocked"),
            (early_rows(total), "blocked"),
            (spectra[-1], "blocked"),
            *[(t, "whole") for t in table["slab_back"]],
            (table["rows_back"], "whole"),
            (total, "whole"),
        ],
        jax.ShapeDtypeStruct(signal.shape, BF16),
        False,
        [work, work],
        rows_flops + 3 * slab_flops,
    )


def spread_kernel(plane, lines, channels, values_ref, out_ref):
    for at in range(plane):
        for line in range(lines):
            first = (at * lines + line) * channels
            out_ref[line, at, 0] = values_ref[0, 0, :, first : first + channels].astype(BF16)


def spread_spectrum(filter_spec, at, first, rows, plane, lines):
    parts, _, _, group_channels = filter_spec.shape
    channels = group_channels // (plane * lines)
    if channels % 128:
        spec = filter_spec[:, at, first : first + rows].reshape(parts, rows, plane, lines, channels)
        return spec.transpose(3, 2, 0, 1, 4).astype(BF16)
    block = max(r for r in range(16, 97, 16) if rows % r == 0 and first % r == 0)
    return pl.pallas_call(
        functools.partial(spread_kernel, plane, lines, channels),
        grid=(parts, rows // block),
        in_specs=[
            pl.BlockSpec((1, 1, block, group_channels), lambda i, j: (i, at, first // block + j, 0))
        ],
        out_specs=pl.BlockSpec((lines, plane, 1, block, channels), lambda i, j: (0, 0, i, j, 0)),
        out_shape=jax.ShapeDtypeStruct((lines, plane, parts, rows, channels), BF16),
        compiler_params=pltpu.CompilerParams(
            dimension_semantics=("arbitrary", "arbitrary"), vmem_limit_bytes=VMEM_LIMIT
        ),
        cost_estimate=pl.CostEstimate(
            flops=0, bytes_accessed=6 * parts * rows * group_channels, transcendentals=0
        ),
        name="spread_spectrum",
    )(filter_spec)


def gate_kernel(lines, channels, values_ref, gate_ref, out_ref):
    for line in range(lines):
        lanes = slice(line * channels, (line + 1) * channels)
        value = gate_ref[:, lanes].astype(F32) * values_ref[line, 0].astype(F32)
        out_ref[:, lanes] = value.astype(BF16)


def gate_output(returned, gate_q, plane, lines):
    _, tok_rows, channels = returned.shape
    returned = returned.reshape(lines, plane, tok_rows, channels)
    if channels % 128:
        returned = returned.transpose(2, 1, 0, 3).reshape(gate_q.shape)
        return (gate_q.astype(F32) * returned.astype(F32)).astype(BF16)
    flat = pl.BlockSpec((tok_rows, lines * channels), lambda i: (0, i))
    return pl.pallas_call(
        functools.partial(gate_kernel, lines, channels),
        grid=(plane,),
        in_specs=[pl.BlockSpec((lines, 1, tok_rows, channels), lambda i: (0, i, 0, 0)), flat],
        out_specs=flat,
        out_shape=jax.ShapeDtypeStruct(gate_q.shape, BF16),
        compiler_params=pltpu.CompilerParams(
            dimension_semantics=("arbitrary",), vmem_limit_bytes=VMEM_LIMIT
        ),
        cost_estimate=pl.CostEstimate(
            flops=gate_q.size, bytes_accessed=6 * gate_q.size, transcendentals=0
        ),
        name="gate_output",
    )(returned, gate_q)


def convolve_plain(signal, spectrum):
    slab_count, tok_rows, channels = signal.shape
    freq_count = 2 * slab_count
    length = freq_count * tok_rows

    def phase(left, right, modulus):
        turns = (left[:, None] * right[None, :] % modulus).astype(F32) * (2.0 * math.pi / modulus)
        return jnp.cos(turns), jnp.sin(turns)

    dot = functools.partial(jnp.einsum, precision=lax.Precision.HIGH, preferred_element_type=F32)
    freq = jnp.arange(freq_count, dtype=jnp.int32)
    slab = jnp.arange(slab_count, dtype=jnp.int32)
    row = jnp.arange(tok_rows, dtype=jnp.int32)
    slab_cos, slab_sin = phase(freq, slab, freq_count)
    turn_cos, turn_sin = (part[:, :, None] for part in phase(freq, row, length))
    row_cos, row_sin = phase(row, row, tok_rows)
    values = signal.astype(F32)
    real, imag = dot("ks,stc->ktc", slab_cos, values), -dot("ks,stc->ktc", slab_sin, values)
    real, imag = real * turn_cos + imag * turn_sin, imag * turn_cos - real * turn_sin
    real, imag = (
        dot("jt,ktc->kjc", row_cos, real) + dot("jt,ktc->kjc", row_sin, imag),
        dot("jt,ktc->kjc", row_cos, imag) - dot("jt,ktc->kjc", row_sin, real),
    )
    spec_real, spec_imag = spectrum[:, 0].astype(F32), spectrum[:, 1].astype(F32)
    real, imag = real * spec_real - imag * spec_imag, imag * spec_real + real * spec_imag
    real, imag = (
        dot("jt,ktc->kjc", row_cos, real) - dot("jt,ktc->kjc", row_sin, imag),
        dot("jt,ktc->kjc", row_cos, imag) + dot("jt,ktc->kjc", row_sin, real),
    )
    real, imag = real * turn_cos - imag * turn_sin, imag * turn_cos + real * turn_sin
    values = dot("ks,ktc->stc", slab_cos, real) - dot("ks,ktc->stc", slab_sin, imag)
    return (values / length).astype(BF16)


def project_kernel(lines, plane, place_ref, *refs):
    along_refs, refs = refs[:lines], refs[lines:]
    feature_refs, refs = refs[: 4 * plane], refs[4 * plane :]
    gate_refs, (out_ref, weight_ref) = refs[:plane], refs[plane:]
    line_at, plane_at, core = place_ref[0], place_ref[1], place_ref[2]
    for k in range(lines):
        line = lax.rem(line_at + lines - k, lines)
        weight_ref[pl.ds(line * plane, plane)] = along_refs[k][...]
    _, weight_rows, wide = weight_ref.shape
    depth = feature_refs[0].shape[1]
    channels = out_ref.shape[3]
    blocks = depth // weight_rows
    for d in range(plane):
        total = None
        for e in range(2):
            for half in range(2):
                first = (2 * lax.rem(core + e, 2) + half) * blocks
                weights = weight_ref[pl.ds(first, blocks)].reshape(depth, wide)
                features = feature_refs[(e * plane + d) * 2 + half][...]
                term = jnp.dot(features, weights, preferred_element_type=F32)
                total = term if total is None else total + term
        value = (gate_refs[d][...].astype(F32) * total).astype(BF16)
        for line in range(lines):
            onward = lax.rem(line + lines - line_at, lines)
            out_ref[onward, plane_at ^ d] = value[:, line * channels : (line + 1) * channels]


def project_fused(place, along, pieces, gates):
    lines, plane = len(along), len(gates)
    _, weight_rows, wide = along[0].shape
    tok_rows = gates[0].shape[0]
    flat = [half for core in pieces for d in core for half in d]
    operands = [*along, *flat, *gates]
    local = pl.BlockSpec(memory_space=pltpu.VMEM)
    return pl.pallas_call(
        functools.partial(project_kernel, lines, plane),
        in_specs=[pl.BlockSpec(memory_space=pltpu.SMEM)] + [local] * len(operands),
        out_specs=local,
        out_shape=jax.ShapeDtypeStruct((lines, plane, tok_rows, wide // lines), BF16),
        scratch_shapes=[pltpu.VMEM((lines * plane, weight_rows, wide), BF16)],
        compiler_params=pltpu.CompilerParams(vmem_limit_bytes=VMEM_LIMIT),
        cost_estimate=pl.CostEstimate(
            flops=2 * wide * sum(f.size for f in flat),
            bytes_accessed=2 * sum(o.size for o in operands),
            transcendentals=0,
        ),
        name="project",
    )(place, *operands)


def project_plain(place, along, pieces, gates):
    line_at, plane_at, core = place[0], place[1], place[2]
    lines = len(along)
    pieces = [jnp.stack([jnp.stack(d) for d in by_core]) for by_core in pieces]
    gates = jnp.stack(gates)
    plane, _, tok_rows, depth = pieces[0].shape
    wide = along[0].shape[2]
    take_line = jnp.mod(line_at - jnp.arange(lines), lines)
    take_plane = jnp.arange(plane) ^ plane_at
    weight = jnp.stack(along)[take_line].reshape(len(pieces), 2, depth, wide)
    total = jnp.zeros((plane, tok_rows, wide), F32)
    for e, piece in enumerate(pieces):
        at = jnp.mod(core - e, len(pieces))
        total += jnp.einsum("phtk,hkc->ptc", piece, weight[at], preferred_element_type=F32)
    value = (gates.astype(F32) * total).astype(BF16)[take_plane]
    value = value.reshape(plane, tok_rows, lines, wide // lines).transpose(2, 0, 1, 3)
    return value[jnp.mod(line_at + jnp.arange(lines), lines)]


def after(values, earlier):
    values, earlier = list(values), list(earlier)
    if not earlier:
        return values
    anywhere = pl.BlockSpec(memory_space=pl.ANY)
    return pl.pallas_call(
        lambda *refs: None,
        in_specs=[anywhere] * (len(values) + len(earlier)),
        out_specs=[anywhere] * len(values),
        out_shape=[jax.ShapeDtypeStruct(v.shape, v.dtype) for v in values],
        input_output_aliases={i: i for i in range(len(values))},
        cost_estimate=pl.CostEstimate(flops=0, bytes_accessed=0, transcendentals=0),
        name="after",
    )(*values, *earlier)


def per_device(tables, features, proj_weight, gate_q, gate_k, filter_spec):
    ctx_size = lax.axis_size("ctx")
    ch_size = lax.axis_size("ch")
    plane = plane_size(ctx_size)
    lines = ctx_size // plane
    me = lax.axis_index("ctx")
    ch_me = lax.axis_index("ch")
    line_at, plane_at = me // plane, me % plane
    tok_rows, feat_cols = features.shape
    weight_rows, group_channels = proj_weight.shape
    wide = group_channels // plane
    channels = wide // lines
    freq_local = filter_spec.shape[1]
    tie = after if channels % 128 == 0 else lambda values, earlier: values

    plane_groups = [[z * plane + p for p in range(plane)] for z in range(lines)]
    onward = [(i, (i + plane) % ctx_size) for i in range(ctx_size)]

    def swap(value, d):
        perm = [(i, i // plane * plane + (i % plane ^ d)) for i in range(ctx_size)]
        return lax.ppermute(value, "ctx", perm)

    def other_core(value, e):
        return lax.ppermute(value, "ch", [(i, (i + e) % ch_size) for i in range(ch_size)])

    def line_shift(value, k):
        return lax.ppermute(value, "ctx", [(i, (i + k * plane) % ctx_size) for i in range(ctx_size)])

    early_rows = tok_rows // 4 // 16 * 16
    early = spread_spectrum(filter_spec, freq_local - 1, 0, early_rows, plane, lines)
    early = [
        lax.dynamic_index_in_dim(early, jnp.mod(line_at + k, lines), 0, keepdims=False)
        for k in range(lines)
    ]
    early = [line_shift(piece, k) if k else piece for k, piece in enumerate(early)]

    weight = proj_weight.reshape(weight_rows, plane, wide).transpose(1, 0, 2)
    weight = lax.all_to_all(weight, "ctx", 0, 0, tiled=True, axis_index_groups=plane_groups)
    along = list(tie([weight], early[1:]))

    halves = jnp.split(features, 2, axis=1)
    held = [{0: half} for half in halves]
    arrival = [[0], [0]]
    bits = [1 << b for b in range(plane.bit_length() - 1)]
    rounds = [
        (turn, k) for turn in range(len(bits)) for k in reversed(range(1 << turn))
    ]

    def feature_round(turn, k, beside):
        ds = [bits[(turn + at) % len(bits)] for at in range(2)]
        sources = [arrival[at][k] for at in range(2)]
        values = [held[at][sources[at]] for at in range(2)]
        if sources[0]:
            values = tie(values, beside)
        new = []
        for at in range(2):
            held[at][sources[at]] = values[at]
            place = sources[at] ^ ds[at]
            held[at][place] = swap(values[at], ds[at])
            new.append(held[at][place])
        if k == 0:
            arrival[:] = [sorted(held[at], key=list(held[at]).index) for at in range(2)]
        return new

    gate_blocks = gate_k.reshape(tok_rows, plane, wide)
    gates = [
        lax.dynamic_index_in_dim(gate_blocks, plane_at ^ d, 1, keepdims=False) for d in range(plane)
    ]
    skipped = [0] * (freq_local - 1) + [early_rows]
    spread = [
        spread_spectrum(filter_spec, at, skip, tok_rows - skip, plane, lines)
        for at, skip in enumerate(skipped)
    ]
    spread = [spec.reshape((ctx_size,) + spec.shape[2:]) for spec in spread]
    beside = []
    for step in range(max(lines - 1, len(rounds))):
        if step < lines - 1:
            along[-1] = tie(along[-1:], beside)[0]
            along.append(lax.ppermute(along[-1], "ctx", onward))
        if step < len(rounds):
            beside = feature_round(*rounds[step], beside + along[step : step + 1])
        beside = beside + spread[step : step + 1] + (gates if step == 1 else [])
    gates = tie(gates, along[-1:])
    gates = [swap(gate, d) if d else gate for d, gate in enumerate(gates)]

    first = tie(spread[:1], along[-1:] + beside)
    spectra = [lax.all_to_all(first[0], "ctx", 0, 0, tiled=True)]

    place = jnp.stack([line_at, plane_at, ch_me]).astype(jnp.int32)
    own = [[held[at][d] for at in range(2)] for d in range(plane)]
    pieces = [own] + [
        [[other_core(half, e) for half in d] for d in own] for e in range(1, ch_size)
    ]
    fits = channels % 128 == 0 and ch_size == 2 and feat_cols // 2 % weight_rows == 0
    if fits and weight_rows % 16 == 0 and tok_rows % 16 == 0:
        projected = project_fused(place, along, pieces, gates)
    else:
        projected = project_plain(place, along, pieces, gates)
    signals = [projected[0]] + [line_shift(projected[k], k) for k in range(1, lines)]

    early = [
        jnp.stack([lax.dynamic_index_in_dim(piece, plane_at ^ d, 0, keepdims=False) for piece in early])
        for d in range(plane)
    ]
    early = tie(early, signals[1:])
    early = [swap(piece, d) if d else piece for d, piece in enumerate(early)]

    def early_spectrum(done):
        stacked = jnp.stack(tie(early, [done]))
        from_plane = (jnp.arange(plane) ^ plane_at)[None, :]
        from_line = jnp.mod(line_at - jnp.arange(lines), lines)[:, None]
        return stacked[from_plane, from_line].reshape((ctx_size,) + stacked.shape[2:])

    for at in range(1, freq_local):
        later = tie(spread[at : at + 1], spectra[-1:] + signals[1:])
        spectra.append(lax.all_to_all(later[0], "ctx", 0, 0, tiled=True))

    if channels % 128 == 0:
        convolved = convolve_fused(place, signals, spectra, tables, early_spectrum)
    else:
        spectra[-1] = jnp.concatenate([early_spectrum(None), spectra[-1]], axis=2)
        spectrum = jnp.stack(spectra, 1).reshape(ctx_size * freq_local, 2, tok_rows, channels)
        signal = jnp.stack(signals)[jnp.mod(line_at - jnp.arange(lines), lines)]
        convolved = convolve_plain(signal.reshape(ctx_size, tok_rows, channels), spectrum)
    returned = lax.all_to_all(convolved, "ctx", 0, 0, tiled=True)
    return gate_output(returned, gate_q, plane, lines)


def solution(mesh):
    ctx_size = mesh.shape["ctx"]

    def whole(features, proj_weight, gate_q, gate_k, filter_spec):
        freq_local = filter_spec.shape[1] // ctx_size
        tables = [
            transform_tables(ctx_size, features.shape[0] // ctx_size, at, freq_local)
            for at in range(freq_local)
        ]
        return jax.shard_map(
            functools.partial(per_device, tables),
            mesh=mesh,
            in_specs=(
                P("ctx", "ch"),
                P("ctx", "ch"),
                P("ctx", "ch"),
                P("ctx", "ch"),
                P(None, "ctx", None, "ch"),
            ),
            out_specs=P("ctx", "ch"),
            check_vma=False,
        )(features, proj_weight, gate_q, gate_k, filter_spec)

    return whole
```
